256 devices in a mesh: rep: 32 (over z_lo, y, core), shard: 8 (over z_hi, x).
Axes of the slice: x: 4, y: 4, z: 8 (z_hi: 2, z_lo: 4; z = z_hi * 4 + z_lo), core: 2. Of those that a mesh axis runs over, the one named last changes fastest.
Arguments:
- master_old: float32 [32, 8, 4608], P('shard'), may hold values from -0.875 to 0.875
- moment_one_old: float32 [32, 8, 4608], P('shard'), may hold values from -0.625 to 0.625
- moment_two_old: float32 [32, 8, 4608], P('shard'), may hold values from 0.002 to 0.05
- grads: bfloat16 [32, 8, 32, 8, 4608], P('rep', 'shard'), may hold values from -0.125 to 0.125
- old_order: int32 [32], replicated, may hold values from 0 to 31, as said below
- new_order: int32 [32], replicated, may hold values from 0 to 31, as said below
- step: int32 [1], replicated, may hold values from 1 to 7
Outputs:
- master_new: float32 [32, 16, 8, 4608], P('rep', 'shard')
- moment_one_new: float32 [32, 16, 8, 4608], P('rep', 'shard')
- moment_two_new: float32 [32, 16, 8, 4608], P('rep', 'shard')
- weights: bfloat16 [32, 32, 8, 4608], P('rep')
The draws below stay inside these ranges and needn't reach their ends.
Inputs may be any that keep to these rules, and one draw needn't show every extreme that they name: old_order and new_order are permutations of the block ids. Of the 4 blocks in the old slots of one old member, at most 1 have their new slot with new members 2 s and 2 s + 1, for every s; this count is reached. `new_order`: a permutation of the block ids, drawn together with old_order.
All inputs are finite; a program needn't handle non-finite values.
Results may differ from the reference program's by a relative error of at most 0.0004.
Values may be sent and summed in bfloat16 or wider, within the bound.
A program may use at most 64 MiB of HBM per device.

```python
import math
import jax
import jax.numpy as jnp
from jax import lax

D = 4608
ROWS = 8
OLD_BLOCKS = 4
BLOCKS = 32
NEW_BLOCKS = 2
N_REP = 32
N_SHARD = 8


def shared_orders(key):
    peers = min(OLD_BLOCKS, N_SHARD)
    capacity = OLD_BLOCKS // peers
    edges = N_SHARD * OLD_BLOCKS
    offsets = jax.random.permutation(jax.random.fold_in(key, 11), N_SHARD)[:peers]
    mapping = jax.random.permutation(jax.random.fold_in(key, 12), N_SHARD)
    senders = jnp.repeat(jnp.arange(N_SHARD, dtype=jnp.int32), OLD_BLOCKS)
    offset_of = jnp.tile(jnp.repeat(offsets.astype(jnp.int32), capacity), N_SHARD)
    target = jnp.take(mapping.astype(jnp.int32), (senders + offset_of) % N_SHARD)
    block_ids = jax.random.permutation(jax.random.fold_in(key, 13), edges).astype(jnp.int32)
    counting = jnp.arange(edges, dtype=jnp.int32)
    old_scores = jax.random.randint(jax.random.fold_in(key, 14), (edges,), 0, 1024) * edges + counting
    old_key = senders * (edges * 1024) + old_scores
    old_rank = jnp.argsort(jnp.argsort(old_key)).astype(jnp.int32)
    new_scores = jax.random.randint(jax.random.fold_in(key, 15), (edges,), 0, 1024) * edges + counting
    new_key = target * (edges * 1024) + new_scores
    new_rank = jnp.argsort(jnp.argsort(new_key)).astype(jnp.int32)
    old_order = jnp.zeros((edges,), jnp.int32).at[old_rank].set(block_ids)
    new_order = jnp.zeros((edges,), jnp.int32).at[new_rank].set(block_ids)
    return (old_order, new_order)


def draw_old_order(key, part):
    return shared_orders(key)[0]


def draw_new_order(key, part):
    return shared_orders(key)[1]


def level_of(stream_key, dims, split, smallest, high):
    level = 1.0
    for position, parts in split:
        draws = jax.random.uniform(jax.random.fold_in(jax.random.fold_in(stream_key, 6), position), (parts,), jnp.float32, smallest / len(split), high / len(split))
        level = level * jnp.repeat(jnp.exp(draws), dims[position] // parts).reshape((-1,) + (1,) * (len(dims) - 1 - position))
    return level


def noise(stream_key, shape, scale, reach, shards=(), kind=jnp.bfloat16):
    gain = level_of(stream_key, shape, shards, -0.22, 0.18) if shards else 1.0
    drawn = jax.random.normal(stream_key, shape, jnp.float32) * scale * gain
    return jnp.minimum(jnp.maximum(drawn, -reach), reach).astype(kind)


def setup_inputs(seed: int = 0) -> dict:
    keys = jax.random.split(jax.random.key(seed), 8)
    master_old = noise(keys[0], (BLOCKS, ROWS, D), 0.15, 0.875, ((0, 8),), jnp.float32)
    moment_one_old = noise(keys[1], (BLOCKS, ROWS, D), 0.1, 0.625, ((0, 8),), jnp.float32)
    moment_two_old = jnp.clip(jnp.exp(math.log(0.05) - 3.218876 * jax.random.uniform(keys[2], (BLOCKS, ROWS, D), jnp.float32) ** level_of(keys[2], (BLOCKS, ROWS, D), ((0, 8),), -0.2, 0.2)), 0.002, 0.05)
    grads = noise(keys[3], (N_REP, N_SHARD, BLOCKS, ROWS, D), 0.02, 0.125, ((0, 32), (1, 8)))
    old_order = draw_old_order(jax.random.fold_in(keys[7], 71), 0)
    new_order = draw_new_order(jax.random.fold_in(keys[7], 71), 0)
    step = jax.random.randint(keys[6], (1,), 1, 8).astype(jnp.int32)
    return dict(master_old=master_old, moment_one_old=moment_one_old, moment_two_old=moment_two_old, grads=grads, old_order=old_order, new_order=new_order, step=step)


def adam_update(master, first, second, grad, step):
    count = step[0].astype(jnp.float32)
    first2 = 0.9 * first + 0.1 * grad
    second2 = 0.95 * second + 0.05 * grad * grad
    fix_one = 1.0 - jnp.power(jnp.float32(0.9), count)
    fix_two = 1.0 - jnp.power(jnp.float32(0.95), count)
    direction = first2 / fix_one / (jnp.sqrt(second2 / fix_two) + 1e-08)
    updated = master - 0.1 * (direction + 0.1 * master)
    return (updated, first2, second2)

def reference(master_old, moment_one_old, moment_two_old, grads, old_order, new_order, step):
    counting = jnp.arange(BLOCKS, dtype=jnp.int32)
    old_slot_of = jnp.zeros((BLOCKS,), jnp.int32).at[old_order].set(counting)
    new_slot_of = jnp.zeros((BLOCKS,), jnp.int32).at[new_order].set(counting)

    def add_replica(total, replica):
        return (total + lax.optimization_barrier(jnp.sum(replica.astype(jnp.float32), axis=0)), None)
    total, _ = lax.scan(add_replica, jnp.zeros((BLOCKS, ROWS, D), jnp.float32), grads)
    source = jnp.take(old_slot_of, new_order, axis=0)
    grad = jnp.take(total, new_order, axis=0)
    master = jnp.take(master_old, source, axis=0)
    first = jnp.take(moment_one_old, source, axis=0)
    second = jnp.take(moment_two_old, source, axis=0)
    updated, first2, second2 = adam_update(master, first, second, grad, step)

    def spread(values):
        halves = values.reshape(N_SHARD, 2, NEW_BLOCKS, ROWS, D)
        paired = jnp.stack([halves[:, 0], halves[:, 1]]).reshape(2, N_SHARD * NEW_BLOCKS, ROWS, D)
        return jnp.tile(paired, (N_REP // 2, 1, 1, 1))
    weights = jnp.take(updated, new_slot_of, axis=0).astype(jnp.bfloat16)
    copies = jnp.tile(weights[None], (N_REP, 1, 1, 1))
    return (spread(updated), spread(first2), spread(second2), copies)
```

```python
import functools

import jax
import jax.numpy as jnp
import numpy as np
from jax import lax
from jax.experimental import pallas as pl
from jax.experimental.pallas import tpu as pltpu
from jax.sharding import PartitionSpec as P

MESH = pl.DeviceIdType.MESH
LANES = 128
F32 = jnp.float32
BF16 = jnp.bfloat16


def power(base, count):
    out = jnp.float32(1.0)
    for bit in range(11):
        factor = np.float32(float(base) ** (1 << bit))
        taken = lax.rem(lax.shift_right_logical(count, jnp.int32(bit)), jnp.int32(2)) == 1
        out = jnp.where(taken, out * factor, out)
    return jnp.where(count >= 2048, jnp.float32(0.0), out)


def kernel(
    dims,
    old_ref, new_ref, step_ref, grads, master, first, second,
    master_out, first_out, second_out, weights_out,
    own, sib, chip, state, state_out, cand,
    send_a, send_b, recv1_a, recv1_b, part_a, part_b, recv2_a, recv2_b,
    half_sum, recv3, result, result_z, other_z, pair, pairs, gathered, ordered,
    send_sem, recv_sem, local_sem,
):
    nx, ny, nzh, nzl, tiles, stop = dims
    nz, ns = nzh * nzl, nzh * nx
    half = tiles * LANES
    part = half // 2
    width = -(-tiles // nzl) * LANES
    starts = [(k * tiles // nzl) * LANES for k in range(nzl + 1)]

    rep, shard = lax.axis_index("rep"), lax.axis_index("shard")
    core = lax.rem(rep, 2)
    y = lax.rem(lax.div(rep, 2), ny)
    zl = lax.div(rep, 2 * ny)
    x, zh = lax.rem(shard, nx), lax.div(shard, nx)
    z = zh * nzl + zl

    def device(x=x, y=y, zh=zh, zl=zl, core=core):
        return ((zl * ny + y) * 2 + core, zh * nx + x)

    def ahead(value, by, size):
        return lax.rem(value + by, size)

    def piece(k):
        return pl.multiple_of(lax.div(k * tiles, nzl) * LANES, LANES)

    count = {"remote": 0, "local": 0}
    sent = []

    def remote(src, dst, to):
        k = count["remote"]
        count["remote"] += 1
        copy = pltpu.make_async_remote_copy(
            src_ref=src, dst_ref=dst, send_sem=send_sem.at[k], recv_sem=recv_sem.at[k],
            device_id=to, device_id_type=MESH,
        )
        copy.start()
        sent.append(copy)
        return copy

    def local(src, dst):
        k = count["local"]
        count["local"] += 1
        copy = pltpu.make_async_copy(src, dst, local_sem.at[k])
        copy.start()
        return copy

    far = lambda n: sorted(range(1, n), key=lambda d: -min(d, n - d))

    mine = pl.multiple_of(core * half, LANES)
    theirs = pl.multiple_of((1 - core) * half, LANES)
    loads = [local(grads.at[:, pl.ds(mine + h * part, part)], own.at[h]) for h in range(2)]
    spot = pl.ds(mine + piece(zl), width)
    state_loads = [local(ref.at[:, :, spot], state.at[k]) for k, ref in enumerate((master, first, second))]

    partners = [device(core=1 - core)]
    partners += [device(x=ahead(x, d, nx)) for d in range(1, nx)]
    partners += [device(y=ahead(y, d, ny)) for d in range(1, ny)]
    for d in range(1, nz):
        other = ahead(z, d, nz)
        partners.append(device(zh=lax.div(other, nzl), zl=lax.rem(other, nzl)))
    for e in range(1, nzh):
        partners += [device(x=ahead(x, d, nx), zh=ahead(zh, e, nzh)) for d in range(1, nx)]
    barrier = pltpu.get_barrier_semaphore()
    for partner in partners:
        pl.semaphore_signal(barrier, inc=1, device_id=partner, device_id_type=MESH)
    pl.semaphore_wait(barrier, len(partners))

    swaps = [
        remote(grads.at[:, pl.ds(theirs + h * part, part)], sib.at[h], device(core=1 - core))
        for h in range(2)
    ]

    for copy in state_loads:
        copy.wait()
    moves = {}
    for e in range(nzh):
        for d in range(nx):
            to_x, to_zh = ahead(x, d, nx), ahead(zh, e, nzh)
            wanted = new_ref[(to_zh * nx + to_x) * ny + y]
            pick = jnp.int32(0)
            for j in range(1, ny):
                pick = jnp.where(old_ref[shard * ny + j] == wanted, jnp.int32(j), pick)
            slot = e * nx + d
            target = cand if slot == 0 else state_out
            for k in range(3):
                target[slot, k] = state[k, pick]
            if slot:
                moves[slot] = remote(state_out.at[slot], cand.at[slot], device(x=to_x, zh=to_zh))

    def chip_sum(h):
        def add(i, carry):
            rows = pl.ds(pl.multiple_of(i * 16, 16), 16)
            both = own[h, rows, :].astype(F32) + sib[h, rows, :].astype(F32)
            chip[h, 2 * i] = both[:8]
            chip[h, 2 * i + 1] = both[8:]
            return carry

        lax.fori_loop(0, ns * ny // 2, add, 0)

    def order(h, buffer, lead, along_x):
        for inner in range(ny if along_x else nx):
            for e in range(nzh):
                to_x, to_y = (lead, inner) if along_x else (inner, lead)
                buffer[lead, inner, e] = chip[h, new_ref[(e * nx + to_x) * ny + to_y]]

    loads[0].wait()
    swaps[0].wait_recv()
    chip_sum(0)
    first_a = {}
    for d in far(nx) + [0]:
        to = ahead(x, d, nx)
        order(0, send_a, to, True)
        if d:
            first_a[d] = remote(send_a.at[to], recv1_a.at[d - 1], device(x=to))
    loads[1].wait()
    swaps[1].wait_recv()
    chip_sum(1)
    first_b = {}
    for d in far(ny) + [0]:
        to = ahead(y, d, ny)
        order(1, send_b, to, False)
        if d:
            first_b[d] = remote(send_b.at[to], recv1_b.at[d - 1], device(y=to))

    for d in range(1, nx):
        first_a[d].wait_recv()
    second_a = {}
    for d in far(ny) + [0]:
        to = ahead(y, d, ny)
        for e in range(nzh):
            total = send_a[x, to, e]
            for q in range(nx - 1):
                total = total + recv1_a[q, to, e]
            part_a[to, e] = total
        if d:
            second_a[d] = remote(part_a.at[to], recv2_a.at[d - 1], device(y=to))
    for d in range(1, ny):
        first_b[d].wait_recv()
    second_b = {}
    for d in far(nx) + [0]:
        to = ahead(x, d, nx)
        for e in range(nzh):
            total = send_b[y, to, e]
            for q in range(ny - 1):
                total = total + recv1_b[q, to, e]
            part_b[to, e] = total
        if d:
            second_b[d] = remote(part_b.at[to], recv2_b.at[d - 1], device(x=to))
    for d in range(1, ny):
        second_a[d].wait_recv()
    for e in range(nzh):
        total = part_a[y, e]
        for q in range(ny - 1):
            total = total + recv2_a[q, e]
        half_sum[e, :, :part] = total
    for d in range(1, nx):
        second_b[d].wait_recv()
    for e in range(nzh):
        total = part_b[x, e]
        for q in range(nx - 1):
            total = total + recv2_b[q, e]
        half_sum[e, :, part:] = total

    third = {}
    for d in far(nz):
        other = ahead(z, d, nz)
        to_zh, to_zl = lax.div(other, nzl), lax.rem(other, nzl)
        third[d] = remote(
            half_sum.at[to_zh, :, pl.ds(piece(to_zl), width)], recv3.at[d - 1], device(zh=to_zh, zl=to_zl)
        )

    wanted = new_ref[shard * ny + y]
    pick = jnp.int32(0)
    for e in range(nzh):
        for d in range(nx):
            slot = e * nx + d
            if slot:
                moves[slot].wait_recv()
                from_x, from_zh = ahead(x, nx - d, nx), ahead(zh, nzh - e, nzh)
                for j in range(ny):
                    match = old_ref[(from_zh * nx + from_x) * ny + j] == wanted
                    pick = jnp.where(match, jnp.int32(slot), pick)
    t = step_ref[0]
    fix_one = 1.0 - power(0.9, t)
    fix_two = 1.0 - power(0.95, t)

    for d in range(1, nz):
        third[d].wait_recv()
    grad = half_sum[zh, :, pl.ds(piece(zl), width)]
    for q in range(nz - 1):
        grad = grad + recv3[q]
    weight = cand[pick, 0]
    moment_one = 0.9 * cand[pick, 1] + 0.1 * grad
    moment_two = 0.95 * cand[pick, 2] + 0.05 * grad * grad
    direction = moment_one / fix_one / (jnp.sqrt(moment_two / fix_two) + 1e-08)
    result[0] = weight - 0.1 * (direction + 0.1 * weight)
    result[1] = moment_one
    result[2] = moment_two

    along = {}
    for e in range(nzh - 1, -1, -1):
        for d in far(nzl) + [0]:
            to = ahead(zl, d, nzl)
            if e:
                along[e, d] = remote(result.at[0], other_z.at[e - 1, zl], device(zh=ahead(zh, e, nzh), zl=to))
            elif d:
                along[e, d] = remote(result, result_z.at[zl], device(zl=to))
    for k in range(3):
        result_z[zl, k] = result[k]
    for copy in along.values():
        copy.wait_recv()
    for k in range(nzl):
        span = starts[k + 1] - starts[k]
        columns = slice(starts[k], starts[k + 1])
        for a in range(3):
            pair[a, :, columns] = result_z[k, a, :, :span]
        same = result_z[k, 0, :, :span]
        rows = []
        for e in range(nzh):
            value = same
            for q in range(1, nzh):
                value = jnp.where(ahead(zh, nzh - q, nzh) == e, other_z[q - 1, k, :, :span], value)
            rows.append(value)
        gathered[x, y, :, columns] = jnp.concatenate(rows, axis=0).astype(BF16)

    over_y = {}
    for d in far(ny):
        over_y[d] = remote(gathered.at[x, y], gathered.at[x, y], device(y=ahead(y, d, ny)))
    pair_y = {}
    for d in far(ny):
        pair_y[d] = remote(pair, pairs.at[y], device(y=ahead(y, d, ny)))
    for a in range(3):
        pairs[y, a] = pair[a]
    for d in range(1, ny):
        over_y[d].wait_recv()

    over_x = {}
    for d in far(nx):
        over_x[d] = remote(gathered.at[x], gathered.at[x], device(x=ahead(x, d, nx)))

    slots = []
    for b in range(ns * ny):
        slot = jnp.int32(0)
        for k in range(1, ns * ny):
            slot = jnp.where(new_ref[k] == b, jnp.int32(k), slot)
        slots.append(slot)
    for d in range(1, ny):
        pair_y[d].wait_recv()
    nb = ny // 2
    outs = []
    for a, ref in enumerate((master_out, first_out, second_out)):
        place = ref.at[:, :, pl.ds(mine, half)]
        outs.append(local(pairs.at[pl.ds(core * nb, nb), a], place))
        remote(pairs.at[pl.ds((1 - core) * nb, nb), a], place, device(core=1 - core))

    for d in range(1, nx):
        over_x[d].wait_recv()
    for i in range(ns * ny // 2):
        rows = []
        for b in (2 * i, 2 * i + 1):
            slot = slots[b]
            at_y, at_x = lax.rem(slot, ny), lax.rem(lax.div(slot, ny), nx)
            at_zh = lax.div(slot, ny * nx)
            block = gathered[at_x, at_y].astype(F32)
            value = block[:8]
            for e in range(1, nzh):
                value = jnp.where(at_zh == e, block[8 * e:8 * e + 8], value)
            rows.append(value)
        ordered[16 * i:16 * i + 16, :] = jnp.concatenate(rows, axis=0).astype(BF16)
    place = weights_out.at[:, pl.ds(mine, half)]
    outs.append(local(ordered, place))
    last = remote(ordered, place, device(core=1 - core))

    for copy in outs:
        copy.wait()
    for copy in sent[-4:]:
        copy.wait_recv()
    for copy in sent:
        copy.wait_send()


def step_call(dims, old_order, new_order, step, grads, master, first, second):
    nx, ny, nzh, nzl, tiles, _ = dims
    nz, ns = nzh * nzl, nzh * nx
    half = tiles * LANES
    part = half // 2
    width = -(-tiles // nzl) * LANES
    blocks = ns * ny
    remotes = 2 + (ns - 1) + 2 * (nx - 1) + 2 * (ny - 1) + 2 * (nz - 1) + 2 * (ny - 1) + (nx - 1) + 4
    vmem = pltpu.VMEM
    f32_out = jax.ShapeDtypeStruct((ny // 2, 8, 2 * half), F32)
    anywhere = pl.BlockSpec(memory_space=pl.ANY)
    scalars = pl.BlockSpec(memory_space=pltpu.SMEM)
    return pl.pallas_call(
        functools.partial(kernel, dims),
        out_shape=(f32_out, f32_out, f32_out, jax.ShapeDtypeStruct((8 * blocks, 2 * half), BF16)),
        in_specs=[scalars] * 3 + [anywhere] * 4,
        out_specs=[anywhere] * 4,
        scratch_shapes=[
            vmem((2, 8 * blocks, part), BF16),
            vmem((2, 8 * blocks, part), BF16),
            vmem((2, blocks, 8, part), F32),
            vmem((3, ny, 8, width), F32),
            vmem((ns, 3, 8, width), F32),
            vmem((ns, 3, 8, width), F32),
            vmem((nx, ny, nzh, 8, part), F32),
            vmem((ny, nx, nzh, 8, part), F32),
            vmem((nx - 1, ny, nzh, 8, part), F32),
            vmem((ny - 1, nx, nzh, 8, part), F32),
            vmem((ny, nzh, 8, part), F32),
            vmem((nx, nzh, 8, part), F32),
            vmem((ny - 1, nzh, 8, part), F32),
            vmem((nx - 1, nzh, 8, part), F32),
            vmem((nzh, 8, half), F32),
            vmem((nz - 1, 8, width), F32),
            vmem((3, 8, width), F32),
            vmem((nzl, 3, 8, width), F32),
            vmem((max(nzh - 1, 1), nzl, 8, width), F32),
            vmem((3, 8, half), F32),
            vmem((ny, 3, 8, half), F32),
            vmem((nx, ny, 8 * nzh, half), BF16),
            vmem((8 * blocks, half), BF16),
            pltpu.SemaphoreType.DMA((remotes,)),
            pltpu.SemaphoreType.DMA((remotes,)),
            pltpu.SemaphoreType.DMA((16,)),
        ],
        compiler_params=pltpu.CompilerParams(
            collective_id=0, has_side_effects=True, vmem_limit_bytes=56 * 1024 * 1024
        ),
        cost_estimate=pl.CostEstimate(flops=4_000_000, bytes_accessed=8_000_000, transcendentals=0),
    )(old_order, new_order, step, grads, master, first, second)


def body(dims, master_old, moment_one_old, moment_two_old, grads, old_order, new_order, step):
    blocks, rows, columns = grads.shape[2:]
    flat = grads.reshape(blocks * rows, columns)
    master, first, second, weights = step_call(
        dims, old_order, new_order, step, flat, master_old, moment_one_old, moment_two_old
    )
    return master[None], first[None], second[None], weights.reshape(1, blocks, rows, columns)


def solution(mesh, dims=(4, 4, 2, 4, 18, 0)):
    return jax.shard_map(
        functools.partial(body, dims),
        mesh=mesh,
        in_specs=(
            P("shard", None, None),
            P("shard", None, None),
            P("shard", None, None),
            P("rep", "shard", None, None, None),
            P(),
            P(),
            P(),
        ),
        out_specs=(
            P("rep", "shard", None, None),
            P("rep", "shard", None, None),
            P("rep", "shard", None, None),
            P("rep", None, None, None),
        ),
        check_vma=False,
    )
```

```python
import functools

import jax
import jax.numpy as jnp
import numpy as np
from jax import lax
from jax.experimental import pallas as pl
from jax.experimental.pallas import tpu as pltpu
from jax.sharding import PartitionSpec as P

MESH = pl.DeviceIdType.MESH
LANES = 128
F32 = jnp.float32
BF16 = jnp.bfloat16


def power(base, count):
    out = jnp.float32(1.0)
    for bit in range(11):
        factor = np.float32(float(base) ** (1 << bit))
        taken = lax.rem(lax.shift_right_logical(count, jnp.int32(bit)), jnp.int32(2)) == 1
        out = jnp.where(taken, out * factor, out)
    return jnp.where(count >= 2048, jnp.float32(0.0), out)


def kernel(
    dims, chunks, stop,
    old_ref, new_ref, step_ref, grads, master, first, second,
    gathered, pairs,
    state, state_out, cand, half_sum, recv3, result, result_z, short, short_z, wide, pair,
    send_sem, recv_sem, pair_sem, local_sem, *buffers,
):
    nx, ny, nzh, nzl, tiles = dims
    nz, ns, nb = nzh * nzl, nzh * nx, ny // 2
    half = tiles * LANES
    width = -(-tiles // nzl) * LANES
    fold = short.shape[1]
    starts = [(k * tiles // nzl) * LANES for k in range(nzl + 1)]

    rep, shard = lax.axis_index("rep"), lax.axis_index("shard")
    core = lax.rem(rep, 2)
    y = lax.rem(lax.div(rep, 2), ny)
    zl = lax.div(rep, 2 * ny)
    x, zh = lax.rem(shard, nx), lax.div(shard, nx)
    z = zh * nzl + zl

    def device(x=x, y=y, zh=zh, zl=zl, core=core):
        return ((zl * ny + y) * 2 + core, zh * nx + x)

    def ahead(value, by, size):
        return lax.rem(value + by, size)

    def piece(k):
        return pl.multiple_of(lax.div(k * tiles, nzl) * LANES, LANES)

    count = {"remote": 0, "local": 0}
    sent = []

    def remote(src, dst, to, sem=None):
        k = count["remote"]
        count["remote"] += 1
        copy = pltpu.make_async_remote_copy(
            src_ref=src, dst_ref=dst, send_sem=send_sem.at[k],
            recv_sem=recv_sem.at[k] if sem is None else sem,
            device_id=to, device_id_type=MESH,
        )
        copy.start()
        sent.append(copy)
        return copy

    def local(src, dst):
        k = count["local"]
        count["local"] += 1
        copy = pltpu.make_async_copy(src, dst, local_sem.at[k])
        copy.start()
        return copy

    def finish():
        for copy in sent:
            copy.wait_send()

    far = lambda n: sorted(range(1, n), key=lambda d: -min(d, n - d))

    parts, column = [], 0
    for k, (along_x, count_tiles) in enumerate(chunks):
        names = ("own", "sib", "chip", "send", "recv1", "part", "recv2")
        refs = dict(zip(names, buffers[len(names) * k:len(names) * (k + 1)]))
        refs.update(along_x=along_x, at=column, size=count_tiles * LANES)
        refs.update(n1=nx if along_x else ny, n2=ny if along_x else nx)
        refs.update(me1=x if along_x else y, me2=y if along_x else x)
        refs.update(axis1="x" if along_x else "y", axis2="y" if along_x else "x")
        parts.append(refs)
        column += count_tiles * LANES

    mine = pl.multiple_of(core * half, LANES)
    theirs = pl.multiple_of((1 - core) * half, LANES)
    for p in parts:
        p["load"] = local(grads.at[:, pl.ds(mine + p["at"], p["size"])], p["own"])
    spot = pl.ds(mine + piece(zl), width)
    state_loads = [local(ref.at[:, :, spot], state.at[k]) for k, ref in enumerate((master, first, second))]

    partners = [device(core=1 - core)]
    partners += [device(x=ahead(x, d, nx)) for d in range(1, nx)]
    for d in range(1, ny):
        partners += [device(y=ahead(y, d, ny)), device(y=ahead(y, d, ny), core=1 - core)]
    for d in range(1, nz):
        other = ahead(z, d, nz)
        partners.append(device(zh=lax.div(other, nzl), zl=lax.rem(other, nzl)))
    for e in range(1, nzh):
        partners += [device(x=ahead(x, d, nx), zh=ahead(zh, e, nzh)) for d in range(1, nx)]
    barrier = pltpu.get_barrier_semaphore()
    for partner in partners:
        pl.semaphore_signal(barrier, inc=1, device_id=partner, device_id_type=MESH)
    pl.semaphore_wait(barrier, len(partners))

    for p in parts:
        p["swap"] = remote(grads.at[:, pl.ds(theirs + p["at"], p["size"])], p["sib"], device(core=1 - core))

    for copy in state_loads:
        copy.wait()
    for e in range(nzh):
        for d in range(nx):
            wanted = new_ref[(ahead(zh, e, nzh) * nx + ahead(x, d, nx)) * ny + y]
            pick = jnp.int32(0)
            for j in range(1, ny):
                pick = jnp.where(old_ref[shard * ny + j] == wanted, jnp.int32(j), pick)
            slot = e * nx + d
            target = state_out if slot else cand
            for k in range(3):
                target[slot, k] = state[k, pick]

    for p in parts:
        p["load"].wait()
        p["swap"].wait_recv()

        def add(i, carry, p=p):
            rows = pl.ds(pl.multiple_of(i * 16, 16), 16)
            both = p["own"][rows, :].astype(F32) + p["sib"][rows, :].astype(F32)
            p["chip"][2 * i] = both[:8]
            p["chip"][2 * i + 1] = both[8:]
            return carry

        lax.fori_loop(0, ns * ny // 2, add, 0)
        p["first"] = {}
        for d in far(p["n1"]) + [0]:
            lead = ahead(p["me1"], d, p["n1"])
            for inner in range(p["n2"]):
                for e in range(nzh):
                    to_x, to_y = (lead, inner) if p["along_x"] else (inner, lead)
                    p["send"][lead, inner, e] = p["chip"][new_ref[(e * nx + to_x) * ny + to_y]]
            if d:
                p["first"][d] = remote(p["send"].at[lead], p["recv1"].at[d - 1], device(**{p["axis1"]: lead}))

    if stop == 2:
        for p in parts:
            for copy in p["first"].values():
                copy.wait_recv()
        return finish()

    moves = {}
    for e in range(nzh - 1, -1, -1):
        for d in far(nx) + [0]:
            slot = e * nx + d
            if slot:
                moves[slot] = remote(
                    state_out.at[slot], cand.at[slot], device(x=ahead(x, d, nx), zh=ahead(zh, e, nzh))
                )

    for p in parts:
        for d in far(p["n1"]):
            p["first"][d].wait_recv()
        p["second"] = {}
        for d in far(p["n2"]) + [0]:
            to = ahead(p["me2"], d, p["n2"])
            for e in range(nzh):
                total = p["send"][p["me1"], to, e]
                for q in range(p["n1"] - 1):
                    total = total + p["recv1"][q, to, e]
                p["part"][to, e] = total
            if d:
                p["second"][d] = remote(p["part"].at[to], p["recv2"].at[d - 1], device(**{p["axis2"]: to}))
    for p in parts:
        for d in far(p["n2"]):
            p["second"][d].wait_recv()
        for e in range(nzh):
            total = p["part"][p["me2"], e]
            for q in range(p["n2"] - 1):
                total = total + p["recv2"][q, e]
            half_sum[e, :, p["at"]:p["at"] + p["size"]] = total

    third = {}
    for d in far(nz):
        other = ahead(z, d, nz)
        to_zh, to_zl = lax.div(other, nzl), lax.rem(other, nzl)
        third[d] = remote(
            half_sum.at[to_zh, :, pl.ds(piece(to_zl), width)], recv3.at[d - 1], device(zh=to_zh, zl=to_zl)
        )

    wanted = new_ref[shard * ny + y]
    pick = jnp.int32(0)
    for e in range(nzh):
        for d in range(nx):
            slot = e * nx + d
            if slot:
                moves[slot].wait_recv()
                from_x, from_zh = ahead(x, nx - d, nx), ahead(zh, nzh - e, nzh)
                for j in range(ny):
                    match = old_ref[(from_zh * nx + from_x) * ny + j] == wanted
                    pick = jnp.where(match, jnp.int32(slot), pick)
    t = step_ref[0]
    fix_one = 1.0 - power(0.9, t)
    fix_two = 1.0 - power(0.95, t)

    if stop == 3:
        for d in range(1, nz):
            third[d].wait_recv()
        return finish()

    for d in far(nz):
        third[d].wait_recv()
    grad = half_sum[zh, :, pl.ds(piece(zl), width)]
    for q in range(nz - 1):
        grad = grad + recv3[q]
    weight = cand[pick, 0]
    moment_one = 0.9 * cand[pick, 1] + 0.1 * grad
    moment_two = 0.95 * cand[pick, 2] + 0.05 * grad * grad
    direction = moment_one / fix_one / (jnp.sqrt(moment_two / fix_two) + 1e-08)
    updated = weight - 0.1 * (direction + 0.1 * weight)

    rest = updated[:, fold:]
    if rest.shape[1] < fold:
        rest = jnp.concatenate([rest, jnp.zeros((8, fold - rest.shape[1]), F32)], axis=1)
    short[...] = jnp.concatenate([updated[:, :fold], rest], axis=0).astype(BF16)
    short_z[z] = short[...]
    over_z = {}
    for d in far(nz):
        other = ahead(z, d, nz)
        over_z[d] = remote(short, short_z.at[z], device(zh=lax.div(other, nzl), zl=lax.rem(other, nzl)))

    for k, value in enumerate((updated, moment_one, moment_two)):
        result[k] = value
        result_z[zl, k] = value
    over_zl = {}
    for d in far(nzl):
        to = ahead(zl, d, nzl)
        over_zl[d] = remote(result, result_z.at[zl], device(zl=to))

    for d in far(nz):
        over_z[d].wait_recv()
    for k in range(nzl):
        span = starts[k + 1] - starts[k]
        for low, high, top in ((0, min(span, fold), 0), (fold, span, 8)):
            if high > low:
                rows = [short_z[e * nzl + k, :, :high - low].astype(F32)[top:top + 8] for e in range(nzh)]
                wide[:, starts[k] + low:starts[k] + high] = jnp.concatenate(rows, axis=0).astype(BF16)
    place = gathered.at[x, y, :, pl.ds(mine, half)]
    over_y = {}
    for d in far(ny):
        over_y[d] = remote(wide, place, device(y=ahead(y, d, ny)))
    kept = local(wide, place)

    for d in far(nzl):
        over_zl[d].wait_recv()
    for k in range(nzl):
        for a in range(3):
            pair[a, :, starts[k]:starts[k + 1]] = result_z[k, a, :, :starts[k + 1] - starts[k]]
    member, row = lax.div(y, nb), lax.rem(y, nb)
    pair_place = pairs.at[:, row, :, pl.ds(mine, half)]
    pair_mark = pair_sem.at[row * 2 + core]
    for d in far(ny):
        remote(pair, pair_place, device(y=ahead(y, d, ny), core=member), pair_mark)
    across = pltpu.make_async_remote_copy(
        src_ref=pair, dst_ref=pair_place, send_sem=send_sem.at[count["remote"]], recv_sem=pair_mark,
        device_id=device(core=1 - core), device_id_type=MESH,
    )
    count["remote"] += 1
    within = pltpu.make_async_copy(pair, pair_place, pair_mark)

    @pl.when(member == core)
    def _():
        within.start()

    @pl.when(member != core)
    def _():
        across.start()

    for d in far(ny):
        over_y[d].wait_recv()
    kept.wait()
    place = gathered.at[x, :, :, pl.ds(mine, half)]
    over_x = {}
    for d in far(nx):
        over_x[d] = remote(place, place, device(x=ahead(x, d, nx)))
    given = [remote(place, place, device(core=1 - core))]
    for d in far(nx)[::-1]:
        over_x[d].wait_recv()
        place = gathered.at[ahead(x, nx - d, nx), :, :, pl.ds(mine, half)]
        given.append(remote(place, place, device(core=1 - core)))

    for r in range(nb):
        for c in range(2):
            pltpu.make_async_copy(pair, pairs.at[:, r, :, pl.ds(c * half, half)], pair_sem.at[r * 2 + c]).wait()

    @pl.when(member != core)
    def _():
        across.wait_send()

    for copy in given:
        copy.wait_recv()
    finish()


def spread_kernel(dims, new_ref, gathered, pairs, master_out, first_out, second_out, weights_out, sem):
    nx, ny, nzh, _, _ = dims
    copies = []
    for a, ref in enumerate((master_out, first_out, second_out)):
        copies.append(pltpu.make_async_copy(pairs.at[a], ref, sem.at[a]))
    for k in range(nzh * nx * ny):
        e, at_x, at_y = k // (nx * ny), k // ny % nx, k % ny
        copies.append(
            pltpu.make_async_copy(gathered.at[(at_x * ny + at_y) * nzh + e], weights_out.at[new_ref[k]], sem.at[3 + k])
        )
    for copy in copies:
        copy.start()
    for copy in copies:
        copy.wait()


def step_call(dims, chunks, stop, old_order, new_order, step, grads, master, first, second):
    nx, ny, nzh, nzl, tiles = dims
    nz, ns, nb = nzh * nzl, nzh * nx, ny // 2
    half = tiles * LANES
    width = -(-tiles // nzl) * LANES
    fold = -(-width // (2 * LANES)) * LANES
    blocks = ns * ny
    remotes = 80
    vmem = pltpu.VMEM
    anywhere = pl.BlockSpec(memory_space=pl.ANY)
    outside = pl.BlockSpec(memory_space=pltpu.HBM)
    scalars = pl.BlockSpec(memory_space=pltpu.SMEM)
    inside = pl.BlockSpec(memory_space=pltpu.VMEM)
    buffers = []
    for along_x, count_tiles in chunks:
        n1, n2 = (nx, ny) if along_x else (ny, nx)
        size = count_tiles * LANES
        buffers += [
            vmem((8 * blocks, size), BF16),
            vmem((8 * blocks, size), BF16),
            vmem((blocks, 8, size), F32),
            vmem((n1, n2, nzh, 8, size), F32),
            vmem((n1 - 1, n2, nzh, 8, size), F32),
            vmem((n2, nzh, 8, size), F32),
            vmem((n2 - 1, nzh, 8, size), F32),
        ]
    gathered, pairs = pl.pallas_call(
        functools.partial(kernel, dims, chunks, stop),
        out_shape=(pltpu.VMEM((nx, ny, 8 * nzh, 2 * half), BF16), pltpu.VMEM((3, nb, 8, 2 * half), F32)),
        in_specs=[scalars] * 3 + [outside] * 4,
        out_specs=[inside] * 2,
        scratch_shapes=[
            vmem((3, ny, 8, width), F32),
            vmem((ns, 3, 8, width), F32),
            vmem((ns, 3, 8, width), F32),
            vmem((nzh, 8, half), F32),
            vmem((nz - 1, 8, width), F32),
            vmem((3, 8, width), F32),
            vmem((nzl, 3, 8, width), F32),
            vmem((16, fold), BF16),
            vmem((nz, 16, fold), BF16),
            vmem((8 * nzh, half), BF16),
            vmem((3, 8, half), F32),
            pltpu.SemaphoreType.DMA((remotes,)),
            pltpu.SemaphoreType.DMA((remotes,)),
            pltpu.SemaphoreType.DMA((2 * nb,)),
            pltpu.SemaphoreType.DMA((16,)),
        ] + buffers,
        compiler_params=pltpu.CompilerParams(
            collective_id=0, has_side_effects=True, vmem_limit_bytes=60 * 1024 * 1024
        ),
        cost_estimate=pl.CostEstimate(flops=4_000_000, bytes_accessed=8_000_000, transcendentals=0),
    )(old_order, new_order, step, grads, master, first, second)
    f32_out = jax.ShapeDtypeStruct((nb, 8, 2 * half), F32)
    return pl.pallas_call(
        functools.partial(spread_kernel, dims),
        out_shape=(f32_out, f32_out, f32_out, jax.ShapeDtypeStruct((blocks, 8, 2 * half), BF16)),
        in_specs=[scalars, inside, inside],
        out_specs=[anywhere] * 4,
        scratch_shapes=[pltpu.SemaphoreType.DMA((3 + blocks,))],
        compiler_params=pltpu.CompilerParams(vmem_limit_bytes=8 * 1024 * 1024),
    )(new_order, gathered.reshape(blocks, 8, 2 * half), pairs)


def body(dims, chunks, stop, master_old, moment_one_old, moment_two_old, grads, old_order, new_order, step):
    blocks, rows, columns = grads.shape[2:]
    flat = grads.reshape(blocks * rows, columns)
    master, first, second, weights = step_call(
        dims, chunks, stop, old_order, new_order, step, flat, master_old, moment_one_old, moment_two_old
    )
    return master[None], first[None], second[None], weights[None]


CHUNKS = ((True, 5), (False, 5), (True, 4), (False, 4))


def solution(mesh, dims=(4, 4, 2, 4, 18), chunks=CHUNKS, stop=0):
    return jax.shard_map(
        functools.partial(body, dims, chunks, stop),
        mesh=mesh,
        in_specs=(
            P("shard", None, None),
            P("shard", None, None),
            P("shard", None, None),
            P("rep", "shard", None, None, None),
            P(),
            P(),
            P(),
        ),
        out_specs=(
            P("rep", "shard", None, None),
            P("rep", "shard", None, None),
            P("rep", "shard", None, None),
            P("rep", None, None, None),
        ),
        check_vma=False,
    )
```

```python
import functools

import jax
import jax.numpy as jnp
import numpy as np
from jax import lax
from jax.experimental import pallas as pl
from jax.experimental.pallas import tpu as pltpu
from jax.sharding import PartitionSpec as P

MESH = pl.DeviceIdType.MESH
LANES = 128
F32 = jnp.float32
BF16 = jnp.bfloat16


def power(base, count):
    out = jnp.float32(1.0)
    for bit in range(11):
        factor = np.float32(float(base) ** (1 << bit))
        taken = lax.rem(lax.shift_right_logical(count, jnp.int32(bit)), jnp.int32(2)) == 1
        out = jnp.where(taken, out * factor, out)
    return jnp.where(count >= 2048, jnp.float32(0.0), out)


def kernel(
    dims, chunks, stop,
    old_ref, new_ref, step_ref, grads, master, first, second,
    gathered, pairs,
    state, state_out, cand, turn, owned, half_sum, recv3, result, result_z, short, short_z, wide, pair,
    send_sem, recv_sem, pair_sem, state_sem, local_sem, *buffers,
):
    nx, ny, nzh, nzl, tiles = dims
    nz, ns, nb = nzh * nzl, nzh * nx, ny // 2
    half = tiles * LANES
    width = -(-tiles // nzl) * LANES
    fold = short.shape[1]
    starts = [(k * tiles // nzl) * LANES for k in range(nzl + 1)]

    rep, shard = lax.axis_index("rep"), lax.axis_index("shard")
    core = lax.rem(rep, 2)
    y = lax.rem(lax.div(rep, 2), ny)
    zl = lax.div(rep, 2 * ny)
    x, zh = lax.rem(shard, nx), lax.div(shard, nx)
    z = zh * nzl + zl

    def device(x=x, y=y, zh=zh, zl=zl, core=core):
        return ((zl * ny + y) * 2 + core, zh * nx + x)

    def ahead(value, by, size):
        return lax.rem(value + by, size)

    def piece(k):
        return pl.multiple_of(lax.div(k * tiles, nzl) * LANES, LANES)

    count = {"remote": 0, "local": 0}
    sent, moves, turns = [], [], []

    def remote(src, dst, to, sem=None):
        k = count["remote"]
        count["remote"] += 1
        copy = pltpu.make_async_remote_copy(
            src_ref=src, dst_ref=dst, send_sem=send_sem.at[k],
            recv_sem=recv_sem.at[k] if sem is None else sem,
            device_id=to, device_id_type=MESH,
        )
        copy.start()
        sent.append(copy)
        return copy

    def local(src, dst):
        k = count["local"]
        count["local"] += 1
        copy = pltpu.make_async_copy(src, dst, local_sem.at[k])
        copy.start()
        return copy

    def finish():
        for copy in sent:
            copy.wait_send()
        for copy in moves:
            pl.when(holds)(copy.wait_send)
        for q, copy in enumerate(turns):
            pl.when(jnp.logical_and(holds, y != q))(copy.wait_send)

    far = lambda n: sorted(range(1, n), key=lambda d: -min(d, n - d))

    parts, column = [], 0
    for k, (along_x, count_tiles) in enumerate(chunks):
        names = ("own", "sib", "chip", "send", "relay", "recv1", "part", "recv2")
        refs = dict(zip(names, buffers[len(names) * k:len(names) * (k + 1)]))
        refs.update(along_x=along_x, at=column, size=count_tiles * LANES)
        refs.update(n1=nx if along_x else ny, n2=ny if along_x else nx)
        refs.update(me1=x if along_x else y, me2=y if along_x else x)
        refs.update(axis1="x" if along_x else "y", axis2="y" if along_x else "x")
        parts.append(refs)
        column += count_tiles * LANES

    mine = pl.multiple_of(core * half, LANES)
    theirs = pl.multiple_of((1 - core) * half, LANES)
    for p in parts:
        p["load"] = local(grads.at[:, pl.ds(mine + p["at"], p["size"])], p["own"])
    spot = pl.ds(mine + piece(zl), width)
    state_loads = [local(ref.at[:, :, spot], state.at[k]) for k, ref in enumerate((master, first, second))]

    partners = [device(core=1 - core)]
    partners += [device(x=ahead(x, d, nx)) for d in range(1, nx)]
    for d in range(1, ny):
        partners += [device(y=ahead(y, d, ny)), device(y=ahead(y, d, ny), core=1 - core)]
    for d in range(1, nz):
        other = ahead(z, d, nz)
        partners.append(device(zh=lax.div(other, nzl), zl=lax.rem(other, nzl)))
    for e in range(1, nzh):
        partners += [device(x=ahead(x, d, nx), zh=ahead(zh, e, nzh)) for d in range(1, nx)]
    barrier = pltpu.get_barrier_semaphore()
    for partner in partners:
        pl.semaphore_signal(barrier, inc=1, device_id=partner, device_id_type=MESH)
    pl.semaphore_wait(barrier, len(partners))

    for p in parts:
        p["swap"] = remote(grads.at[:, pl.ds(theirs + p["at"], p["size"])], p["sib"], device(core=1 - core))

    for copy in state_loads:
        copy.wait()
    holds = y < 3
    kind = jnp.where(holds, y, 2)
    for e in range(nzh - 1, -1, -1):
        for d in far(nx) + [0]:
            to_x, to_zh = ahead(x, d, nx), ahead(zh, e, nzh)
            to_slot = (to_zh * nx + to_x) * ny
            pick = jnp.int32(0)
            for j in range(1, ny):
                block = old_ref[shard * ny + j]
                for q in range(ny):
                    pick = jnp.where(new_ref[to_slot + q] == block, jnp.int32(j), pick)
            slot = e * nx + d
            target = state_out if slot else cand
            target[slot] = state[kind, pick]
            if slot:
                copy = pltpu.make_async_remote_copy(
                    src_ref=state_out.at[slot], dst_ref=cand.at[slot],
                    send_sem=state_sem.at[0, slot], recv_sem=state_sem.at[1, slot],
                    device_id=device(x=to_x, zh=to_zh), device_id_type=MESH,
                )
                moves.append(copy)
                pl.when(holds)(copy.start)

    def chip_sum(p):
        p["load"].wait()
        p["swap"].wait_recv()

        def add(i, carry):
            rows = pl.ds(pl.multiple_of(i * 16, 16), 16)
            both = p["own"][rows, :].astype(F32) + p["sib"][rows, :].astype(F32)
            p["chip"][2 * i] = both[:8]
            p["chip"][2 * i + 1] = both[8:]
            return carry

        lax.fori_loop(0, ns * ny // 2, add, 0)

    def order(p, lead):
        for inner in range(p["n2"]):
            for e in range(nzh):
                to_x, to_y = (lead, inner) if p["along_x"] else (inner, lead)
                p["send"][lead, inner, e] = p["chip"][new_ref[(e * nx + to_x) * ny + to_y]]

    def first_step(p):
        chip_sum(p)
        n, me, h = p["n1"], p["me1"], p["n2"] // 2
        low, high = pl.ds(0, h), pl.ds(h, h)
        up, down = ahead(me, 1, n), ahead(me, n - 1, n)
        if n == 2:
            order(p, up)
            p["got"] = [remote(p["send"].at[up], p["recv1"].at[0], device(**{p["axis1"]: up}))]
            order(p, me)
            return
        to_up, to_down = device(**{p["axis1"]: up}), device(**{p["axis1"]: down})
        across = ahead(me, 2, n)
        order(p, across)
        p["relays"] = [
            remote(p["send"].at[across, low], p["relay"].at[0], to_up),
            remote(p["send"].at[across, high], p["relay"].at[1], to_down),
        ]
        order(p, up)
        p["got"] = [remote(p["send"].at[up, high], p["recv1"].at[0, high], to_up)]
        order(p, down)
        p["got"].append(remote(p["send"].at[down, low], p["recv1"].at[1, low], to_down))
        order(p, me)

    def second_step(p):
        n, me, h = p["n1"], p["me1"], p["n2"] // 2
        if n == 2:
            return
        low, high = pl.ds(0, h), pl.ds(h, h)
        up, down = ahead(me, 1, n), ahead(me, n - 1, n)
        to_up, to_down = device(**{p["axis1"]: up}), device(**{p["axis1"]: down})
        p["relays"][0].wait_recv()
        p["send"][up, low] = p["send"][up, low] + p["relay"][0]
        p["got"].append(remote(p["send"].at[up, low], p["recv1"].at[0, low], to_up))
        p["relays"][1].wait_recv()
        p["send"][down, high] = p["send"][down, high] + p["relay"][1]
        p["got"].append(remote(p["send"].at[down, high], p["recv1"].at[1, high], to_down))

    for k, p in enumerate(parts):
        first_step(p)
        if k >= 2:
            second_step(parts[k - 2])
    for p in parts[-2:]:
        second_step(p)

    if stop == 2:
        for p in parts:
            for copy in p["got"]:
                copy.wait_recv()
        for copy in moves:
            pl.when(holds)(copy.wait_recv)
        return finish()

    picks = []
    for q in range(ny):
        wanted = new_ref[shard * ny + q]
        pick = jnp.int32(0)
        for e in range(nzh):
            for d in range(nx):
                if e or d:
                    from_x, from_zh = ahead(x, nx - d, nx), ahead(zh, nzh - e, nzh)
                    for j in range(ny):
                        match = old_ref[(from_zh * nx + from_x) * ny + j] == wanted
                        pick = jnp.where(match, jnp.int32(e * nx + d), pick)
        picks.append(pick)
    for copy in moves:
        pl.when(holds)(copy.wait_recv)
    for q in range(ny):
        turn[q] = cand[picks[q]]
        copy = pltpu.make_async_remote_copy(
            src_ref=turn.at[q], dst_ref=owned.at[kind],
            send_sem=state_sem.at[2, q], recv_sem=state_sem.at[3, kind],
            device_id=device(y=q), device_id_type=MESH,
        )
        turns.append(copy)
        pl.when(jnp.logical_and(holds, y != q))(copy.start)

    @pl.when(holds)
    def _():
        owned[kind] = turn[y]

    for p in parts:
        for copy in p["got"]:
            copy.wait_recv()
        p["second"] = {}
        for d in far(p["n2"]) + [0]:
            to = ahead(p["me2"], d, p["n2"])
            for e in range(nzh):
                total = p["send"][p["me1"], to, e]
                for q in range(min(p["n1"] - 1, 2)):
                    total = total + p["recv1"][q, to, e]
                p["part"][to, e] = total
            if d:
                p["second"][d] = remote(p["part"].at[to], p["recv2"].at[d - 1], device(**{p["axis2"]: to}))
    for p in parts:
        for d in far(p["n2"]):
            p["second"][d].wait_recv()
        for e in range(nzh):
            total = p["part"][p["me2"], e]
            for q in range(p["n2"] - 1):
                total = total + p["recv2"][q, e]
            half_sum[e, :, p["at"]:p["at"] + p["size"]] = total

    third = {}
    for d in far(nz):
        other = ahead(z, d, nz)
        to_zh, to_zl = lax.div(other, nzl), lax.rem(other, nzl)
        third[d] = remote(
            half_sum.at[to_zh, :, pl.ds(piece(to_zl), width)], recv3.at[d - 1], device(zh=to_zh, zl=to_zl)
        )

    for k in range(3):
        copy = pltpu.make_async_copy(owned.at[k], owned.at[k], state_sem.at[3, k])
        pl.when(y != k)(copy.wait)
    t = step_ref[0]
    fix_one = 1.0 - power(0.9, t)
    fix_two = 1.0 - power(0.95, t)

    if stop == 3:
        for d in range(1, nz):
            third[d].wait_recv()
        return finish()

    for d in far(nz):
        third[d].wait_recv()
    grad = half_sum[zh, :, pl.ds(piece(zl), width)]
    for q in range(nz - 1):
        grad = grad + recv3[q]
    weight = owned[0]
    moment_one = 0.9 * owned[1] + 0.1 * grad
    moment_two = 0.95 * owned[2] + 0.05 * grad * grad
    direction = moment_one / fix_one / (jnp.sqrt(moment_two / fix_two) + 1e-08)
    updated = weight - 0.1 * (direction + 0.1 * weight)

    rest = updated[:, fold:]
    if rest.shape[1] < fold:
        rest = jnp.concatenate([rest, jnp.zeros((8, fold - rest.shape[1]), F32)], axis=1)
    short[...] = jnp.concatenate([updated[:, :fold], rest], axis=0).astype(BF16)
    short_z[z] = short[...]
    over_z = {}
    for d in far(nz):
        other = ahead(z, d, nz)
        over_z[d] = remote(short, short_z.at[z], device(zh=lax.div(other, nzl), zl=lax.rem(other, nzl)))

    for k, value in enumerate((updated, moment_one, moment_two)):
        result[k] = value
        result_z[zl, k] = value
    over_zl = {}
    for d in far(nzl):
        to = ahead(zl, d, nzl)
        over_zl[d] = remote(result, result_z.at[zl], device(zl=to))

    for d in far(nz):
        over_z[d].wait_recv()
    for k in range(nzl):
        span = starts[k + 1] - starts[k]
        for low, high, top in ((0, min(span, fold), 0), (fold, span, 8)):
            if high > low:
                rows = [short_z[e * nzl + k, :, :high - low].astype(F32)[top:top + 8] for e in range(nzh)]
                wide[:, starts[k] + low:starts[k] + high] = jnp.concatenate(rows, axis=0).astype(BF16)
    place = gathered.at[x, y, :, pl.ds(mine, half)]
    over_y = {}
    for d in far(ny):
        over_y[d] = remote(wide, place, device(y=ahead(y, d, ny)))
    kept = local(wide, place)

    for d in far(nzl):
        over_zl[d].wait_recv()
    for k in range(nzl):
        for a in range(3):
            pair[a, :, starts[k]:starts[k + 1]] = result_z[k, a, :, :starts[k + 1] - starts[k]]
    member, row = lax.div(y, nb), lax.rem(y, nb)
    pair_place = pairs.at[:, row, :, pl.ds(mine, half)]
    pair_mark = pair_sem.at[row * 2 + core]
    for d in far(ny):
        remote(pair, pair_place, device(y=ahead(y, d, ny), core=member), pair_mark)
    across = pltpu.make_async_remote_copy(
        src_ref=pair, dst_ref=pair_place, send_sem=send_sem.at[count["remote"]], recv_sem=pair_mark,
        device_id=device(core=1 - core), device_id_type=MESH,
    )
    count["remote"] += 1
    within = pltpu.make_async_copy(pair, pair_place, pair_mark)

    @pl.when(member == core)
    def _():
        within.start()

    @pl.when(member != core)
    def _():
        across.start()

    for d in far(ny):
        over_y[d].wait_recv()
    kept.wait()
    place = gathered.at[x, :, :, pl.ds(mine, half)]
    n, h = nx, ny // 2
    low, high = pl.ds(0, h), pl.ds(h, h)
    up, down = ahead(x, 1, n), ahead(x, n - 1, n)

    def quarter(of, rows):
        return gathered.at[of, rows, :, pl.ds(mine, half)]

    def pass_on(of, rows, to):
        return remote(quarter(of, rows), quarter(of, rows), to)

    sibling = device(core=1 - core)
    if n == 2:
        comes = [pass_on(x, pl.ds(0, ny), device(x=up))]
        given = [pass_on(x, pl.ds(0, ny), sibling)]
        comes[0].wait_recv()
        given.append(pass_on(up, pl.ds(0, ny), sibling))
    else:
        to_up, to_down = device(x=up), device(x=down)
        from_down, from_up = [pass_on(x, low, to_up)], [pass_on(x, high, to_down)]
        from_down.append(pass_on(x, high, to_up))
        from_up.append(pass_on(x, low, to_down))
        given = [pass_on(x, pl.ds(0, ny), sibling)]
        from_down[0].wait_recv()
        far_low = pass_on(down, low, to_up)
        from_up[0].wait_recv()
        far_high = pass_on(up, high, to_down)
        given += [pass_on(down, low, sibling), pass_on(up, high, sibling)]
        from_down[1].wait_recv()
        given.append(pass_on(down, high, sibling))
        from_up[1].wait_recv()
        given.append(pass_on(up, low, sibling))
        across_x = ahead(x, 2, n)
        far_low.wait_recv()
        given.append(pass_on(across_x, low, sibling))
        far_high.wait_recv()
        given.append(pass_on(across_x, high, sibling))

    for r in range(nb):
        for c in range(2):
            pltpu.make_async_copy(pair, pairs.at[:, r, :, pl.ds(c * half, half)], pair_sem.at[r * 2 + c]).wait()

    @pl.when(member != core)
    def _():
        across.wait_send()

    for copy in given:
        copy.wait_recv()
    finish()


def spread_kernel(dims, new_ref, gathered, pairs, master_out, first_out, second_out, weights_out, sem):
    nx, ny, nzh, _, _ = dims
    copies = []
    for a, ref in enumerate((master_out, first_out, second_out)):
        copies.append(pltpu.make_async_copy(pairs.at[a], ref, sem.at[a]))
    for k in range(nzh * nx * ny):
        e, at_x, at_y = k // (nx * ny), k // ny % nx, k % ny
        copies.append(
            pltpu.make_async_copy(gathered.at[(at_x * ny + at_y) * nzh + e], weights_out.at[new_ref[k]], sem.at[3 + k])
        )
    for copy in copies:
        copy.start()
    for copy in copies:
        copy.wait()


def step_call(dims, chunks, stop, old_order, new_order, step, grads, master, first, second):
    nx, ny, nzh, nzl, tiles = dims
    nz, ns, nb = nzh * nzl, nzh * nx, ny // 2
    half = tiles * LANES
    width = -(-tiles // nzl) * LANES
    fold = -(-width // (2 * LANES)) * LANES
    blocks = ns * ny
    remotes = 80
    vmem = pltpu.VMEM
    anywhere = pl.BlockSpec(memory_space=pl.ANY)
    outside = pl.BlockSpec(memory_space=pltpu.HBM)
    scalars = pl.BlockSpec(memory_space=pltpu.SMEM)
    inside = pl.BlockSpec(memory_space=pltpu.VMEM)
    buffers = []
    for along_x, count_tiles in chunks:
        n1, n2 = (nx, ny) if along_x else (ny, nx)
        size = count_tiles * LANES
        buffers += [
            vmem((8 * blocks, size), BF16),
            vmem((8 * blocks, size), BF16),
            vmem((blocks, 8, size), F32),
            vmem((n1, n2, nzh, 8, size), F32),
            vmem((2, n2 // 2, nzh, 8, size), F32),
            vmem((min(n1 - 1, 2), n2, nzh, 8, size), F32),
            vmem((n2, nzh, 8, size), F32),
            vmem((n2 - 1, nzh, 8, size), F32),
        ]
    gathered, pairs = pl.pallas_call(
        functools.partial(kernel, dims, chunks, stop),
        out_shape=(pltpu.VMEM((nx, ny, 8 * nzh, 2 * half), BF16), pltpu.VMEM((3, nb, 8, 2 * half), F32)),
        in_specs=[scalars] * 3 + [outside] * 4,
        out_specs=[inside] * 2,
        scratch_shapes=[
            vmem((3, ny, 8, width), F32),
            vmem((ns, 8, width), F32),
            vmem((ns, 8, width), F32),
            vmem((ny, 8, width), F32),
            vmem((3, 8, width), F32),
            vmem((nzh, 8, half), F32),
            vmem((nz - 1, 8, width), F32),
            vmem((3, 8, width), F32),
            vmem((nzl, 3, 8, width), F32),
            vmem((16, fold), BF16),
            vmem((nz, 16, fold), BF16),
            vmem((8 * nzh, half), BF16),
            vmem((3, 8, half), F32),
            pltpu.SemaphoreType.DMA((remotes,)),
            pltpu.SemaphoreType.DMA((remotes,)),
            pltpu.SemaphoreType.DMA((2 * nb,)),
            pltpu.SemaphoreType.DMA((4, ns)),
            pltpu.SemaphoreType.DMA((16,)),
        ] + buffers,
        compiler_params=pltpu.CompilerParams(
            collective_id=0, has_side_effects=True, vmem_limit_bytes=60 * 1024 * 1024
        ),
        cost_estimate=pl.CostEstimate(flops=4_000_000, bytes_accessed=8_000_000, transcendentals=0),
    )(old_order, new_order, step, grads, master, first, second)
    f32_out = jax.ShapeDtypeStruct((nb, 8, 2 * half), F32)
    return pl.pallas_call(
        functools.partial(spread_kernel, dims),
        out_shape=(f32_out, f32_out, f32_out, jax.ShapeDtypeStruct((blocks, 8, 2 * half), BF16)),
        in_specs=[scalars, inside, inside],
        out_specs=[anywhere] * 4,
        scratch_shapes=[pltpu.SemaphoreType.DMA((3 + blocks,))],
        compiler_params=pltpu.CompilerParams(vmem_limit_bytes=8 * 1024 * 1024),
    )(new_order, gathered.reshape(blocks, 8, 2 * half), pairs)


def body(dims, chunks, stop, master_old, moment_one_old, moment_two_old, grads, old_order, new_order, step):
    blocks, rows, columns = grads.shape[2:]
    flat = grads.reshape(blocks * rows, columns)
    master, first, second, weights = step_call(
        dims, chunks, stop, old_order, new_order, step, flat, master_old, moment_one_old, moment_two_old
    )
    return master[None], first[None], second[None], weights[None]


CHUNKS = ((True, 5), (False, 5), (True, 4), (False, 4))


def solution(mesh, dims=(4, 4, 2, 4, 18), chunks=CHUNKS, stop=0):
    return jax.shard_map(
        functools.partial(body, dims, chunks, stop),
        mesh=mesh,
        in_specs=(
            P("shard", None, None),
            P("shard", None, None),
            P("shard", None, None),
            P("rep", "shard", None, None, None),
            P(),
            P(),
            P(),
        ),
        out_specs=(
            P("rep", "shard", None, None),
            P("rep", "shard", None, None),
            P("rep", "shard", None, None),
            P("rep", None, None, None),
        ),
        check_vma=False,
    )
```

```python
import functools
from types import SimpleNamespace

import jax
import jax.numpy as jnp
import numpy as np
from jax import lax
from jax.experimental import pallas as pl
from jax.experimental.pallas import tpu as pltpu
from jax.sharding import PartitionSpec as P

MESH = pl.DeviceIdType.MESH
LANES = 128
MARKS = 91
F32 = jnp.float32
BF16 = jnp.bfloat16


def power(base, count):
    out = jnp.float32(1.0)
    for bit in range(11):
        factor = np.float32(float(base) ** (1 << bit))
        taken = lax.rem(lax.shift_right_logical(count, jnp.int32(bit)), jnp.int32(2)) == 1
        out = jnp.where(taken, out * factor, out)
    return jnp.where(count >= 2048, jnp.float32(0.0), out)


def kernel(
    dims, groups, stop,
    old_in, new_in, step_in, grads, master, first, second,
    gathered, pairs,
    old_ref, new_ref, step_ref,
    state, state_out, cand, turn, owned,
    sems, *buffers,
):
    nx, ny, nzh, nzl, tiles = dims
    nz, ns, nb = nzh * nzl, nzh * nx, ny // 2
    half = tiles * LANES

    rep, shard = lax.axis_index("rep"), lax.axis_index("shard")
    core = lax.rem(rep, 2)
    y = lax.rem(lax.div(rep, 2), ny)
    zl = lax.div(rep, 2 * ny)
    x, zh = lax.rem(shard, nx), lax.div(shard, nx)
    z = zh * nzl + zl

    def device(x=x, y=y, zh=zh, zl=zl, core=core):
        return ((zl * ny + y) * 2 + core, zh * nx + x)

    def on_x(to):
        return device(x=to)

    def on_y(to):
        return device(y=to)

    def ahead(value, by, size):
        return lax.rem(value + by, size)

    used = []
    ends = []

    def mark():
        used.append(1)
        return sems.at[len(used) - 1]

    def take(ref, sem):
        pltpu.make_async_copy(ref, ref, sem).wait()

    def remote(src, dst, to, send, recv, when=None):
        copy = pltpu.make_async_remote_copy(
            src_ref=src, dst_ref=dst, send_sem=send, recv_sem=recv, device_id=to, device_id_type=MESH
        )
        if when is None:
            copy.start()
        else:
            pl.when(when)(copy.start)

    def local(src, dst, sem):
        copy = pltpu.make_async_copy(src, dst, sem)
        copy.start()
        return copy

    def sends(ref, when=None):
        sem = mark()
        ends.append((ref, sem, when))
        return sem

    def finish():
        for ref, sem, when in ends:
            if when is None:
                take(ref, sem)
            else:
                pl.when(when)(functools.partial(take, ref, sem))

    far = lambda n: sorted(range(1, n), key=lambda d: -min(d, n - d))
    mine = pl.multiple_of(core * half, LANES)
    theirs = pl.multiple_of((1 - core) * half, LANES)
    sibling = device(core=1 - core)

    teams, column, k = [], 0, 0
    for chunks in groups:
        g = SimpleNamespace(at=column, parts=[], tiles=sum(n for _, n in chunks))
        inner = 0
        for along_x, count_tiles in chunks:
            p = SimpleNamespace(along_x=along_x, at=column + inner, inner=inner, size=count_tiles * LANES)
            p.own, p.sib, p.chip, p.send, p.relay, p.recv1, p.part, p.recv2 = buffers[k:k + 8]
            k += 8
            p.n1, p.n2, p.me1, p.me2 = (nx, ny, x, y) if along_x else (ny, nx, y, x)
            p.to1, p.to2 = (on_x, on_y) if along_x else (on_y, on_x)
            inner += count_tiles * LANES
            g.parts.append(p)
        g.sum, g.recv3, g.result, g.result_z, g.short, g.short_z, g.wide, g.pair = buffers[k:k + 8]
        k += 8
        g.size = inner
        g.width = g.result.shape[2]
        g.fold = g.short.shape[1]
        g.starts = [(q * g.tiles // nzl) * LANES for q in range(nzl + 1)]
        column += inner
        teams.append(g)

    def piece(g, q):
        return pl.multiple_of(lax.div(q * g.tiles, nzl) * LANES, LANES)

    small = [local(src, dst, mark()) for src, dst in ((old_in, old_ref), (new_in, new_ref), (step_in, step_ref))]
    for g in teams:
        for p in g.parts:
            p.load = local(grads.at[:, pl.ds(mine + p.at, p.size)], p.own, mark())
    state_mark, column = mark(), 0
    for g in teams:
        g.state_at = column
        for a, ref in enumerate((master, first, second)):
            spot = pl.ds(mine + g.at + piece(g, zl), g.width)
            local(ref.at[:, :, spot], state.at[a, :, :, pl.ds(column, g.width)], state_mark)
        column += g.width

    partners = [sibling]
    partners += [device(x=ahead(x, d, nx)) for d in range(1, nx)]
    for d in range(1, ny):
        partners += [device(y=ahead(y, d, ny)), device(y=ahead(y, d, ny), core=1 - core)]
    for d in range(1, nz):
        other = ahead(z, d, nz)
        partners.append(device(zh=lax.div(other, nzl), zl=lax.rem(other, nzl)))
    for e in range(1, nzh):
        partners += [device(x=ahead(x, d, nx), zh=ahead(zh, e, nzh)) for d in range(1, nx)]
    barrier = pltpu.get_barrier_semaphore()
    for partner in partners:
        pl.semaphore_signal(barrier, inc=1, device_id=partner, device_id_type=MESH)
    pl.semaphore_wait(barrier, len(partners))

    swap_send = sends(grads.at[:, pl.ds(0, half)])
    for g in teams:
        for p in g.parts:
            p.swap = mark()
            remote(grads.at[:, pl.ds(theirs + p.at, p.size)], p.sib, sibling, swap_send, p.swap)

    holds = y < 3
    kind = jnp.where(holds, y, 2)
    moved = state_out.at[pl.ds(1, ns - 1)]
    move_send, move_recv = sends(moved, holds), mark()
    turn_marks = [mark() for _ in range(3)]
    turn_send = mark()
    turn_recv = sems.at[kind + (len(used) - 4)]
    ends.append((turn.at[pl.ds(0, ny - 1)], turn_send, holds))

    def state_first():
        take(state, state_mark)
        for e in range(nzh - 1, -1, -1):
            for d in far(nx) + [0]:
                to_x, to_zh = ahead(x, d, nx), ahead(zh, e, nzh)
                to_slot = (to_zh * nx + to_x) * ny
                pick = jnp.int32(0)
                for j in range(1, ny):
                    block = old_ref[shard * ny + j]
                    for q in range(ny):
                        pick = jnp.where(new_ref[to_slot + q] == block, jnp.int32(j), pick)
                slot = e * nx + d
                target = state_out if slot else cand
                target[slot] = state[kind, pick]
                if slot:
                    to = device(x=to_x, zh=to_zh)
                    remote(state_out.at[slot], cand.at[slot], to, move_send, move_recv, holds)

    def state_second():
        picks = []
        for q in range(ny):
            wanted = new_ref[shard * ny + q]
            pick = jnp.int32(0)
            for e in range(nzh):
                for d in range(nx):
                    if e or d:
                        from_x, from_zh = ahead(x, nx - d, nx), ahead(zh, nzh - e, nzh)
                        for j in range(ny):
                            match = old_ref[(from_zh * nx + from_x) * ny + j] == wanted
                            pick = jnp.where(match, jnp.int32(e * nx + d), pick)
            picks.append(pick)
        pl.when(holds)(functools.partial(take, moved, move_recv))
        for q in range(ny):
            turn[q] = cand[picks[q]]
            away = jnp.logical_and(holds, y != q)
            remote(turn.at[q], owned.at[kind], device(y=q), turn_send, turn_recv, away)

        @pl.when(holds)
        def _():
            owned[kind] = turn[y]

    def state_done():
        for a in range(3):
            pl.when(y != a)(functools.partial(take, owned.at[a], turn_marks[a]))

    def chip_sum(p):
        p.load.wait()
        take(p.sib, p.swap)

        def add(i, carry):
            rows = pl.ds(pl.multiple_of(i * 16, 16), 16)
            both = p.own[rows, :].astype(F32) + p.sib[rows, :].astype(F32)
            p.chip[2 * i] = both[:8]
            p.chip[2 * i + 1] = both[8:]
            return carry

        lax.fori_loop(0, ns * ny // 2, add, 0)

    def order(p, lead):
        for inner in range(p.n2):
            for e in range(nzh):
                to_x, to_y = (lead, inner) if p.along_x else (inner, lead)
                p.send[lead, inner, e] = p.chip[new_ref[(e * nx + to_x) * ny + to_y]]

    def first_step(p):
        chip_sum(p)
        n, me, h = p.n1, p.me1, p.n2 // 2
        low, high = pl.ds(0, h), pl.ds(h, h)
        up, down = ahead(me, 1, n), ahead(me, n - 1, n)
        if n == 2:
            order(p, up)
            p.got = mark()
            remote(p.send.at[up], p.recv1.at[0], p.to1(up), sends(p.send.at[0]), p.got)
            order(p, me)
            return
        to_up, to_down = p.to1(up), p.to1(down)
        across = ahead(me, 2, n)
        order(p, across)
        p.relays, p.got, p.out = [mark(), mark()], mark(), sends(p.send.at[pl.ds(0, 3)])
        out, got = p.out, p.got
        remote(p.send.at[across, low], p.relay.at[0], to_up, out, p.relays[0])
        remote(p.send.at[across, high], p.relay.at[1], to_down, out, p.relays[1])
        order(p, up)
        remote(p.send.at[up, high], p.recv1.at[0, high], to_up, out, got)
        order(p, down)
        remote(p.send.at[down, low], p.recv1.at[1, low], to_down, out, got)
        order(p, me)

    def second_step(p):
        n, me, h = p.n1, p.me1, p.n2 // 2
        if n == 2:
            return
        low, high = pl.ds(0, h), pl.ds(h, h)
        up, down = ahead(me, 1, n), ahead(me, n - 1, n)
        to_up, to_down = p.to1(up), p.to1(down)
        take(p.relay.at[0], p.relays[0])
        p.send[up, low] = p.send[up, low] + p.relay[0]
        remote(p.send.at[up, low], p.recv1.at[0, low], to_up, p.out, p.got)
        take(p.relay.at[1], p.relays[1])
        p.send[down, high] = p.send[down, high] + p.relay[1]
        remote(p.send.at[down, high], p.recv1.at[1, high], to_down, p.out, p.got)

    def third_step(p):
        take(p.recv1, p.got)
        p.second, out = mark(), sends(p.recv2)
        for d in far(p.n2) + [0]:
            to = ahead(p.me2, d, p.n2)
            for e in range(nzh):
                total = p.send[p.me1, to, e]
                for q in range(min(p.n1 - 1, 2)):
                    total = total + p.recv1[q, to, e]
                p.part[to, e] = total
            if d:
                remote(p.part.at[to], p.recv2.at[d - 1], p.to2(to), out, p.second)

    def sum_z(g):
        for p in g.parts:
            take(p.recv2, p.second)
            for e in range(nzh):
                total = p.part[p.me2, e]
                for q in range(p.n2 - 1):
                    total = total + p.recv2[q, e]
                g.sum[e, :, p.inner:p.inner + p.size] = total
        g.third, out = mark(), sends(g.recv3)
        for d in far(nz):
            other = ahead(z, d, nz)
            to_zh, to_zl = lax.div(other, nzl), lax.rem(other, nzl)
            src = g.sum.at[to_zh, :, pl.ds(piece(g, to_zl), g.width)]
            remote(src, g.recv3.at[d - 1], device(zh=to_zh, zl=to_zl), out, g.third)

    def update(g, fix_one, fix_two):
        take(g.recv3, g.third)
        grad = g.sum[zh, :, pl.ds(piece(g, zl), g.width)]
        for q in range(nz - 1):
            grad = grad + g.recv3[q]
        spot = slice(g.state_at, g.state_at + g.width)
        weight = owned[0, :, spot]
        moment_one = 0.9 * owned[1, :, spot] + 0.1 * grad
        moment_two = 0.95 * owned[2, :, spot] + 0.05 * grad * grad
        direction = moment_one / fix_one / (jnp.sqrt(moment_two / fix_two) + 1e-08)
        updated = weight - 0.1 * (direction + 0.1 * weight)
        fold, short, short_z = g.fold, g.short, g.short_z
        rest = updated[:, fold:]
        if rest.shape[1] < fold:
            rest = jnp.concatenate([rest, jnp.zeros((8, fold - rest.shape[1]), F32)], axis=1)
        short[...] = jnp.concatenate([updated[:, :fold], rest], axis=0).astype(BF16)
        g.over_z, out = mark(), sends(short_z.at[pl.ds(0, nz - 1)])
        for d in far(nz):
            other = ahead(z, d, nz)
            to = device(zh=lax.div(other, nzl), zl=lax.rem(other, nzl))
            remote(short, short_z.at[z], to, out, g.over_z)
        short_z[z] = short[...]
        for a, value in enumerate((updated, moment_one, moment_two)):
            g.result[a] = value
            g.result_z[zl, a] = value

    def block_place(g, of_x, of_y):
        return gathered.at[of_x, of_y, :, pl.ds(mine + g.at, g.size)]

    def weights_y(g):
        take(g.short_z.at[pl.ds(0, nz - 1)], g.over_z)
        starts, fold = g.starts, g.fold
        for q in range(nzl):
            span = starts[q + 1] - starts[q]
            for low, high, top in ((0, min(span, fold), 0), (fold, span, 8)):
                if high > low:
                    rows = [g.short_z[e * nzl + q, :, :high - low].astype(F32)[top:top + 8] for e in range(nzh)]
                    g.wide[:, starts[q] + low:starts[q] + high] = jnp.concatenate(rows, axis=0).astype(BF16)
        place = block_place(g, x, y)
        rest = gathered.at[0, pl.ds(0, ny - 1), :, pl.ds(0, g.size)]
        g.over_y, out = mark(), sends(rest)
        for d in far(ny):
            remote(g.wide, place, device(y=ahead(y, d, ny)), out, g.over_y)
        g.kept = local(g.wide, place, mark())

    def masters_z(g):
        if nzl > 1:
            g.over_zl, out = mark(), sends(g.result_z.at[pl.ds(0, nzl - 1)])
        for d in far(nzl):
            remote(g.result, g.result_z.at[zl], device(zl=ahead(zl, d, nzl)), out, g.over_zl)

    member, row = lax.div(y, nb), lax.rem(y, nb)

    def pairs_y(g):
        if nzl > 1:
            take(g.result_z.at[pl.ds(0, nzl - 1)], g.over_zl)
        starts = g.starts
        for q in range(nzl):
            for a in range(3):
                g.pair[a, :, starts[q]:starts[q + 1]] = g.result_z[q, a, :, :starts[q + 1] - starts[q]]
        place = pairs.at[:, row, :, pl.ds(mine + g.at, g.size)]
        first_mark = len(used)
        g.pair_marks = [mark() for _ in range(2 * nb)]
        landed = sems.at[first_mark + row * 2 + core]
        for d in far(ny):
            remote(g.pair, place, device(y=ahead(y, d, ny), core=member), sends(g.pair), landed)
        remote(g.pair, place, sibling, sends(g.pair, member != core), landed, member != core)
        within = pltpu.make_async_copy(g.pair, place, landed)
        pl.when(member == core)(within.start)

    def pairs_done(g):
        for k in range(2 * nb):
            take(g.pair, g.pair_marks[k])

    h = ny // 2
    low, high = pl.ds(0, h), pl.ds(h, h)
    up, down = ahead(x, 1, nx), ahead(x, nx - 1, nx)

    def pass_on(g, of, rows, to, send, recv):
        place = gathered.at[of, rows, :, pl.ds(mine + g.at, g.size)]
        remote(place, place, to, send, recv)

    def span(g, of, rows):
        return gathered.at[of, rows, :, pl.ds(0, g.size)]

    every = pl.ds(0, ny)

    def weights_x(g):
        take(span(g, 0, pl.ds(0, ny - 1)), g.over_y)
        g.kept.wait()
        g.given, g.give = mark(), sends(span(g, pl.ds(0, nx), every))
        if nx == 2:
            g.near = mark()
            pass_on(g, x, every, device(x=up), sends(span(g, 0, every)), g.near)
            pass_on(g, x, every, sibling, g.give, g.given)
            return
        to_up, to_down = device(x=up), device(x=down)
        g.out = sends(span(g, pl.ds(0, 3), every))
        g.come = [mark(), mark()]
        g.near = mark()
        pass_on(g, x, low, to_up, g.out, g.come[0])
        pass_on(g, x, high, to_down, g.out, g.come[1])
        pass_on(g, x, high, to_up, g.out, g.near)
        pass_on(g, x, low, to_down, g.out, g.near)
        pass_on(g, x, every, sibling, g.give, g.given)

    def weights_on(g):
        if nx == 2:
            return
        g.far = mark()
        take(span(g, 0, low), g.come[0])
        pass_on(g, down, low, device(x=up), g.out, g.far)
        take(span(g, 0, high), g.come[1])
        pass_on(g, up, high, device(x=down), g.out, g.far)
        pass_on(g, down, low, sibling, g.give, g.given)
        pass_on(g, up, high, sibling, g.give, g.given)

    def weights_last(g):
        take(span(g, 0, every), g.near)
        if nx == 2:
            pass_on(g, up, every, sibling, g.give, g.given)
            return
        pass_on(g, down, high, sibling, g.give, g.given)
        pass_on(g, up, low, sibling, g.give, g.given)
        take(span(g, 0, every), g.far)
        pass_on(g, ahead(x, 2, nx), every, sibling, g.give, g.given)

    for copy in small:
        copy.wait()
    one, two = teams
    (a0, b0), (a1, b1) = one.parts, two.parts
    first_step(a0)
    first_step(b0)
    first_step(a1)
    first_step(b1)
    second_step(a0)
    second_step(b0)
    state_first()
    t = step_ref[0]
    fix_one = 1.0 - power(0.9, t)
    fix_two = 1.0 - power(0.95, t)
    second_step(a1)
    second_step(b1)
    third_step(a0)
    third_step(b0)
    state_second()
    third_step(a1)
    third_step(b1)
    sum_z(one)
    sum_z(two)
    state_done()
    update(one, fix_one, fix_two)
    update(two, fix_one, fix_two)
    weights_y(one)
    masters_z(one)
    weights_y(two)
    masters_z(two)
    weights_x(one)
    weights_x(two)
    pairs_y(one)
    weights_on(one)
    pairs_y(two)
    weights_on(two)
    weights_last(one)
    weights_last(two)
    for g in teams:
        pairs_done(g)
        take(span(g, pl.ds(0, nx), every), g.given)
    finish()


def spread_kernel(dims, new_in, gathered, pairs, master_out, first_out, second_out, weights_out, new_ref, sem):
    nx, ny, nzh, _, _ = dims
    order = pltpu.make_async_copy(new_in, new_ref, sem.at[0])
    order.start()
    copies = []
    for a, ref in enumerate((master_out, first_out, second_out)):
        copies.append(pltpu.make_async_copy(pairs.at[a], ref, sem.at[1 + a]))
        copies[-1].start()
    order.wait()
    for k in range(nzh * nx * ny):
        e, at_x, at_y = k // (nx * ny), k // ny % nx, k % ny
        copy = (
            pltpu.make_async_copy(gathered.at[(at_x * ny + at_y) * nzh + e], weights_out.at[new_ref[k]], sem.at[4])
        )
        copy.start()
    for copy in copies:
        copy.wait()
    pltpu.make_async_copy(gathered, gathered, sem.at[4]).wait()


def step_call(dims, groups, stop, old_order, new_order, step, grads, master, first, second):
    nx, ny, nzh, nzl, tiles = dims
    nz, ns, nb = nzh * nzl, nzh * nx, ny // 2
    half = tiles * LANES
    blocks = ns * ny
    vmem = pltpu.VMEM
    anywhere = pl.BlockSpec(memory_space=pl.ANY)
    outside = pl.BlockSpec(memory_space=pltpu.HBM)
    inside = pl.BlockSpec(memory_space=pltpu.VMEM)
    buffers, state_width = [], 0
    for chunks in groups:
        for along_x, count_tiles in chunks:
            n1, n2 = (nx, ny) if along_x else (ny, nx)
            size = count_tiles * LANES
            buffers += [
                vmem((8 * blocks, size), BF16),
                vmem((8 * blocks, size), BF16),
                vmem((blocks, 8, size), F32),
                vmem((n1, n2, nzh, 8, size), F32),
                vmem((2, n2 // 2, nzh, 8, size), F32),
                vmem((min(n1 - 1, 2), n2, nzh, 8, size), F32),
                vmem((n2, nzh, 8, size), F32),
                vmem((n2 - 1, nzh, 8, size), F32),
            ]
        group_tiles = sum(n for _, n in chunks)
        size = group_tiles * LANES
        width = -(-group_tiles // nzl) * LANES
        fold = -(-width // (2 * LANES)) * LANES
        state_width += width
        buffers += [
            vmem((nzh, 8, size), F32),
            vmem((nz - 1, 8, width), F32),
            vmem((3, 8, width), F32),
            vmem((nzl, 3, 8, width), F32),
            vmem((16, fold), BF16),
            vmem((nz, 16, fold), BF16),
            vmem((8 * nzh, size), BF16),
            vmem((3, 8, size), F32),
        ]
    gathered, pairs = pl.pallas_call(
        functools.partial(kernel, dims, groups, stop),
        out_shape=(pltpu.VMEM((nx, ny, 8 * nzh, 2 * half), BF16), pltpu.VMEM((3, nb, 8, 2 * half), F32)),
        in_specs=[anywhere] * 3 + [outside] * 4,
        out_specs=[inside] * 2,
        scratch_shapes=[
            pltpu.SMEM((blocks,), jnp.int32),
            pltpu.SMEM((blocks,), jnp.int32),
            pltpu.SMEM((1,), jnp.int32),
            vmem((3, ny, 8, state_width), F32),
            vmem((ns, 8, state_width), F32),
            vmem((ns, 8, state_width), F32),
            vmem((ny, 8, state_width), F32),
            vmem((3, 8, state_width), F32),
            pltpu.SemaphoreType.DMA((MARKS,)),
        ] + buffers,
        compiler_params=pltpu.CompilerParams(
            collective_id=0, has_side_effects=True, vmem_limit_bytes=60 * 1024 * 1024
        ),
        cost_estimate=pl.CostEstimate(flops=4_000_000, bytes_accessed=8_000_000, transcendentals=0),
    )(old_order, new_order, step, grads, master, first, second)
    f32_out = jax.ShapeDtypeStruct((nb, 8, 2 * half), F32)
    return pl.pallas_call(
        functools.partial(spread_kernel, dims),
        out_shape=(f32_out, f32_out, f32_out, jax.ShapeDtypeStruct((blocks, 8, 2 * half), BF16)),
        in_specs=[anywhere, inside, inside],
        out_specs=[anywhere] * 4,
        scratch_shapes=[pltpu.SMEM((blocks,), jnp.int32), pltpu.SemaphoreType.DMA((5,))],
        compiler_params=pltpu.CompilerParams(vmem_limit_bytes=8 * 1024 * 1024),
    )(new_order, gathered.reshape(blocks, 8, 2 * half), pairs)


def body(dims, groups, stop, master_old, moment_one_old, moment_two_old, grads, old_order, new_order, step):
    blocks, rows, columns = grads.shape[2:]
    flat = grads.reshape(blocks * rows, columns)
    master, first, second, weights = step_call(
        dims, groups, stop, old_order, new_order, step, flat, master_old, moment_one_old, moment_two_old
    )
    return master[None], first[None], second[None], weights[None]


GROUPS = (((True, 5), (False, 4)), ((True, 4), (False, 5)))


def solution(mesh, dims=(4, 4, 2, 4, 18), groups=GROUPS, stop=0):
    return jax.shard_map(
        functools.partial(body, dims, groups, stop),
        mesh=mesh,
        in_specs=(
            P("shard", None, None),
            P("shard", None, None),
            P("shard", None, None),
            P("rep", "shard", None, None, None),
            P(),
            P(),
            P(),
        ),
        out_specs=(
            P("rep", "shard", None, None),
            P("rep", "shard", None, None),
            P("rep", "shard", None, None),
            P("rep", None, None, None),
        ),
        check_vma=False,
    )
```

```python
import functools
from types import SimpleNamespace

import jax
import jax.numpy as jnp
import numpy as np
from jax import lax
from jax.experimental import pallas as pl
from jax.experimental.pallas import tpu as pltpu
from jax.sharding import PartitionSpec as P

MESH = pl.DeviceIdType.MESH
LANES = 128
MARKS = 97
F32 = jnp.float32
BF16 = jnp.bfloat16


def power(base, count):
    out = jnp.float32(1.0)
    for bit in range(11):
        factor = np.float32(float(base) ** (1 << bit))
        taken = lax.rem(lax.shift_right_logical(count, jnp.int32(bit)), jnp.int32(2)) == 1
        out = jnp.where(taken, out * factor, out)
    return jnp.where(count >= 2048, jnp.float32(0.0), out)


def kernel(
    dims, groups, stop,
    old_in, new_in, step_in, grads, master, first, second,
    gathered, pairs, new_out,
    old_ref, new_ref, step_ref,
    state, state_out, cand, turn, owned,
    sems, *buffers,
):
    nx, ny, nzh, nzl, tiles = dims
    nz, ns, nb = nzh * nzl, nzh * nx, ny // 2
    half = tiles * LANES

    rep, shard = lax.axis_index("rep"), lax.axis_index("shard")
    core = lax.rem(rep, 2)
    y = lax.rem(lax.div(rep, 2), ny)
    zl = lax.div(rep, 2 * ny)
    x, zh = lax.rem(shard, nx), lax.div(shard, nx)
    z = zh * nzl + zl

    def device(x=x, y=y, zh=zh, zl=zl, core=core):
        return ((zl * ny + y) * 2 + core, zh * nx + x)

    def on_x(to):
        return device(x=to)

    def on_y(to):
        return device(y=to)

    def ahead(value, by, size):
        return lax.rem(value + by, size)

    used = []
    ends = []

    def mark():
        used.append(1)
        return sems.at[len(used) - 1]

    def take(ref, sem):
        pltpu.make_async_copy(ref, ref, sem).wait()

    def remote(src, dst, to, send, recv, when=None):
        copy = pltpu.make_async_remote_copy(
            src_ref=src, dst_ref=dst, send_sem=send, recv_sem=recv, device_id=to, device_id_type=MESH
        )
        if when is None:
            copy.start()
        else:
            pl.when(when)(copy.start)

    def local(src, dst, sem):
        copy = pltpu.make_async_copy(src, dst, sem)
        copy.start()
        return copy

    def sends(ref, when=None):
        sem = mark()
        ends.append((ref, sem, when))
        return sem

    def finish():
        for ref, sem, when in ends:
            if when is None:
                take(ref, sem)
            else:
                pl.when(when)(functools.partial(take, ref, sem))

    far = lambda n: sorted(range(1, n), key=lambda d: -min(d, n - d))
    mine = pl.multiple_of(core * half, LANES)
    theirs = pl.multiple_of((1 - core) * half, LANES)
    sibling = device(core=1 - core)

    teams, column, k = [], 0, 0
    for chunks in groups:
        g = SimpleNamespace(at=column, parts=[], tiles=sum(n for _, n in chunks))
        inner = 0
        for along_x, count_tiles in chunks:
            p = SimpleNamespace(along_x=along_x, at=column + inner, inner=inner, size=count_tiles * LANES)
            p.own, p.sib, p.chip, p.send, p.relay, p.recv1, p.part, p.recv2 = buffers[k:k + 8]
            k += 8
            p.n1, p.n2, p.me1, p.me2 = (nx, ny, x, y) if along_x else (ny, nx, y, x)
            p.to1, p.to2 = (on_x, on_y) if along_x else (on_y, on_x)
            inner += count_tiles * LANES
            g.parts.append(p)
        g.sum, g.recv3, g.result, g.result_z, g.short, g.short_z, g.wide, g.pair = buffers[k:k + 8]
        k += 8
        g.size = inner
        g.width = g.result.shape[2]
        g.fold = g.short.shape[1]
        g.starts = [(q * g.tiles // nzl) * LANES for q in range(nzl + 1)]
        column += inner
        teams.append(g)

    def piece(g, q):
        return pl.multiple_of(lax.div(q * g.tiles, nzl) * LANES, LANES)

    small = [local(src, dst, mark()) for src, dst in ((old_in, old_ref), (new_in, new_ref), (step_in, step_ref))]
    for g in teams:
        for p in g.parts:
            p.load = local(grads.at[:, pl.ds(mine + p.at, p.size)], p.own, mark())
    state_mark, column = mark(), 0
    for g in teams:
        g.state_at = column
        for a, ref in enumerate((master, first, second)):
            spot = pl.ds(mine + g.at + piece(g, zl), g.width)
            local(ref.at[:, :, spot], state.at[a, :, :, pl.ds(column, g.width)], state_mark)
        column += g.width

    partners = [sibling]
    partners += [device(x=ahead(x, d, nx)) for d in range(1, nx)]
    for d in range(1, ny):
        partners += [device(y=ahead(y, d, ny)), device(y=ahead(y, d, ny), core=1 - core)]
    for d in range(1, nz):
        other = ahead(z, d, nz)
        partners.append(device(zh=lax.div(other, nzl), zl=lax.rem(other, nzl)))
    for e in range(1, nzh):
        partners += [device(x=ahead(x, d, nx), zh=ahead(zh, e, nzh)) for d in range(1, nx)]
    barrier = pltpu.get_barrier_semaphore()
    for partner in partners:
        pl.semaphore_signal(barrier, inc=1, device_id=partner, device_id_type=MESH)
    pl.semaphore_wait(barrier, len(partners))

    swap_send = sends(grads.at[:, pl.ds(0, half)])

    def swap(g):
        for p in g.parts:
            p.swap = mark()
            remote(grads.at[:, pl.ds(theirs + p.at, p.size)], p.sib, sibling, swap_send, p.swap)


    holds = y < 3
    kind = jnp.where(holds, y, 2)
    moved = state_out.at[pl.ds(1, ns - 1)]
    move_send, move_recv = sends(moved, holds), mark()
    turn_marks = [mark() for _ in range(3)]
    turn_send = mark()
    turn_recv = sems.at[kind + (len(used) - 4)]
    ends.append((turn.at[pl.ds(0, ny - 1)], turn_send, holds))

    def state_first():
        take(state, state_mark)
        for e in range(nzh - 1, -1, -1):
            for d in far(nx) + [0]:
                to_x, to_zh = ahead(x, d, nx), ahead(zh, e, nzh)
                to_slot = (to_zh * nx + to_x) * ny
                pick = jnp.int32(0)
                for j in range(1, ny):
                    block = old_ref[shard * ny + j]
                    for q in range(ny):
                        pick = jnp.where(new_ref[to_slot + q] == block, jnp.int32(j), pick)
                slot = e * nx + d
                target = state_out if slot else cand
                target[slot] = state[kind, pick]
                if slot:
                    to = device(x=to_x, zh=to_zh)
                    remote(state_out.at[slot], cand.at[slot], to, move_send, move_recv, holds)

    def state_second():
        picks = []
        for q in range(ny):
            wanted = new_ref[shard * ny + q]
            pick = jnp.int32(0)
            for e in range(nzh):
                for d in range(nx):
                    if e or d:
                        from_x, from_zh = ahead(x, nx - d, nx), ahead(zh, nzh - e, nzh)
                        for j in range(ny):
                            match = old_ref[(from_zh * nx + from_x) * ny + j] == wanted
                            pick = jnp.where(match, jnp.int32(e * nx + d), pick)
            picks.append(pick)
        pl.when(holds)(functools.partial(take, moved, move_recv))
        for q in range(ny):
            turn[q] = cand[picks[q]]
            away = jnp.logical_and(holds, y != q)
            remote(turn.at[q], owned.at[kind], device(y=q), turn_send, turn_recv, away)

        @pl.when(holds)
        def _():
            owned[kind] = turn[y]

    def state_done():
        for a in range(3):
            pl.when(y != a)(functools.partial(take, owned.at[a], turn_marks[a]))

    def chip_sum(p):
        p.load.wait()
        take(p.sib, p.swap)

        def add(i, carry):
            rows = pl.ds(pl.multiple_of(i * 16, 16), 16)
            both = p.own[rows, :].astype(F32) + p.sib[rows, :].astype(F32)
            p.chip[2 * i] = both[:8]
            p.chip[2 * i + 1] = both[8:]
            return carry

        lax.fori_loop(0, ns * ny // 2, add, 0)

    def order(p, lead):
        for inner in range(p.n2):
            for e in range(nzh):
                to_x, to_y = (lead, inner) if p.along_x else (inner, lead)
                p.send[lead, inner, e] = p.chip[new_ref[(e * nx + to_x) * ny + to_y]]

    def first_step(p):
        chip_sum(p)
        n, me, h = p.n1, p.me1, p.n2 // 2
        low, high = pl.ds(0, h), pl.ds(h, h)
        up, down = ahead(me, 1, n), ahead(me, n - 1, n)
        if n == 2:
            order(p, up)
            p.got = mark()
            remote(p.send.at[up], p.recv1.at[0], p.to1(up), sends(p.send.at[0]), p.got)
            order(p, me)
            return
        to_up, to_down = p.to1(up), p.to1(down)
        across = ahead(me, 2, n)
        order(p, across)
        p.relays, p.got, p.out = [mark(), mark()], mark(), sends(p.send.at[pl.ds(0, 3)])
        out, got = p.out, p.got
        remote(p.send.at[across, low], p.relay.at[0], to_up, out, p.relays[0])
        remote(p.send.at[across, high], p.relay.at[1], to_down, out, p.relays[1])
        order(p, up)
        remote(p.send.at[up, high], p.recv1.at[0, high], to_up, out, got)
        order(p, down)
        remote(p.send.at[down, low], p.recv1.at[1, low], to_down, out, got)
        order(p, me)

    def second_step(p):
        n, me, h = p.n1, p.me1, p.n2 // 2
        if n == 2:
            return
        low, high = pl.ds(0, h), pl.ds(h, h)
        up, down = ahead(me, 1, n), ahead(me, n - 1, n)
        to_up, to_down = p.to1(up), p.to1(down)
        take(p.relay.at[0], p.relays[0])
        p.send[up, low] = p.send[up, low] + p.relay[0]
        remote(p.send.at[up, low], p.recv1.at[0, low], to_up, p.out, p.got)
        take(p.relay.at[1], p.relays[1])
        p.send[down, high] = p.send[down, high] + p.relay[1]
        remote(p.send.at[down, high], p.recv1.at[1, high], to_down, p.out, p.got)

    def third_step(p):
        take(p.recv1, p.got)
        p.second, out = mark(), sends(p.recv2)
        for d in far(p.n2) + [0]:
            to = ahead(p.me2, d, p.n2)
            for e in range(nzh):
                total = p.send[p.me1, to, e]
                for q in range(min(p.n1 - 1, 2)):
                    total = total + p.recv1[q, to, e]
                p.part[to, e] = total
            if d:
                remote(p.part.at[to], p.recv2.at[d - 1], p.to2(to), out, p.second)

    def sum_z(g):
        for p in g.parts:
            take(p.recv2, p.second)
            for e in range(nzh):
                total = p.part[p.me2, e]
                for q in range(p.n2 - 1):
                    total = total + p.recv2[q, e]
                g.sum[e, :, p.inner:p.inner + p.size] = total
        g.third, out = mark(), sends(g.recv3)
        for d in far(nz):
            other = ahead(z, d, nz)
            to_zh, to_zl = lax.div(other, nzl), lax.rem(other, nzl)
            src = g.sum.at[to_zh, :, pl.ds(piece(g, to_zl), g.width)]
            remote(src, g.recv3.at[d - 1], device(zh=to_zh, zl=to_zl), out, g.third)

    def update(g, fix_one, fix_two):
        take(g.recv3, g.third)
        grad = g.sum[zh, :, pl.ds(piece(g, zl), g.width)]
        for q in range(nz - 1):
            grad = grad + g.recv3[q]
        spot = slice(g.state_at, g.state_at + g.width)
        weight = owned[0, :, spot]
        moment_one = 0.9 * owned[1, :, spot] + 0.1 * grad
        moment_two = 0.95 * owned[2, :, spot] + 0.05 * grad * grad
        direction = moment_one / fix_one / (jnp.sqrt(moment_two / fix_two) + 1e-08)
        updated = weight - 0.1 * (direction + 0.1 * weight)
        fold, short, short_z = g.fold, g.short, g.short_z
        rest = updated[:, fold:]
        if rest.shape[1] < fold:
            rest = jnp.concatenate([rest, jnp.zeros((8, fold - rest.shape[1]), F32)], axis=1)
        short[...] = jnp.concatenate([updated[:, :fold], rest], axis=0).astype(BF16)
        g.over_z, out = mark(), sends(short_z.at[pl.ds(0, nz - 1)])
        for d in far(nz):
            other = ahead(z, d, nz)
            to = device(zh=lax.div(other, nzl), zl=lax.rem(other, nzl))
            remote(short, short_z.at[z], to, out, g.over_z)
        short_z[z] = short[...]
        for a, value in enumerate((updated, moment_one, moment_two)):
            g.result[a] = value
            g.result_z[zl, a] = value

    every = pl.ds(0, ny)
    up, down = ahead(x, 1, nx), ahead(x, nx - 1, nx)

    def extent(g, of, rows):
        return gathered.at[of, rows, :, pl.ds(0, g.size)]

    def block_place(g, of_x, of_y):
        return gathered.at[of_x, of_y, :, pl.ds(mine + g.at, g.size)]

    def weights_y(g):
        take(g.short_z.at[pl.ds(0, nz - 1)], g.over_z)
        starts, fold = g.starts, g.fold
        for q in range(nzl):
            span = starts[q + 1] - starts[q]
            for low, high, top in ((0, min(span, fold), 0), (fold, span, 8)):
                if high > low:
                    rows = [g.short_z[e * nzl + q, :, :high - low].astype(F32)[top:top + 8] for e in range(nzh)]
                    g.wide[:, starts[q] + low:starts[q] + high] = jnp.concatenate(rows, axis=0).astype(BF16)
        place = block_place(g, x, y)
        g.over_y, out = mark(), sends(extent(g, 0, pl.ds(0, ny - 1)))
        g.out = sends(extent(g, pl.ds(0, 3), every))
        g.come, g.near, g.far = [mark() for _ in range(4)], mark(), mark()
        remote(g.wide, place, device(x=up), g.out, g.come[0])
        remote(g.wide, place, device(x=down), g.out, g.near)
        for d in far(ny):
            remote(g.wide, place, device(y=ahead(y, d, ny)), out, g.over_y)
        g.kept = local(g.wide, place, mark())

    def masters_z(g):
        g.over_zl = [mark() for _ in range(nzl)]
        landed = sems.at[len(used) - nzl + zl]
        if nzl > 1:
            out = sends(g.result_z.at[pl.ds(0, nzl - 1)])
        for d in far(nzl):
            remote(g.result, g.result_z.at[zl], device(zl=ahead(zl, d, nzl)), out, landed)

    member, row = lax.div(y, nb), lax.rem(y, nb)

    def hand_out(g, q, src, when):
        at, wide = g.starts[q], g.starts[q + 1] - g.starts[q]
        src = src.at[:, :, pl.ds(0, wide)]
        place = pairs.at[:, row, :, pl.ds(mine + g.at + at, wide)]
        for d in far(ny):
            remote(src, place, device(y=ahead(y, d, ny), core=member), g.pair_out, g.landed, when)
        remote(src, place, sibling, g.pair_give, g.landed, jnp.logical_and(when, member != core))
        within = pltpu.make_async_copy(src, place, g.landed)
        pl.when(jnp.logical_and(when, member == core))(within.start)

    def pairs_own(g):
        g.pair_marks = [mark() for _ in range(2 * nb)]
        g.landed = sems.at[len(used) - 2 * nb + row * 2 + core]
        g.pair_out = sends(pairs.at[:, 0, :, pl.ds(0, (ny - 1) * g.size)])
        g.pair_give = sends(g.pair, member != core)
        for q in range(nzl):
            hand_out(g, q, g.result, zl == q)

    def pairs_y(g):
        for q in range(nzl):
            pl.when(zl != q)(functools.partial(take, g.result_z.at[q], g.over_zl[q]))
            hand_out(g, q, g.result_z.at[q], zl != q)

    def pairs_done(g):
        for k in range(2 * nb):
            take(g.pair, g.pair_marks[k])

    def pass_on(g, of, rows, to, send, recv):
        place = gathered.at[of, rows, :, pl.ds(mine + g.at, g.size)]
        remote(place, place, to, send, recv)

    def weights_x(g):
        to_up, to_down = device(x=up), device(x=down)
        block = extent(g, 0, 0)
        rows = [ahead(y, j, ny) for j in range(ny)]
        take(block, g.come[0])
        pass_on(g, down, rows[0], to_up, g.out, g.far)
        take(extent(g, 0, pl.ds(0, ny - 1)), g.over_y)
        g.kept.wait()
        pass_on(g, x, rows[1], to_up, g.out, g.come[1])
        pass_on(g, x, rows[2], to_down, g.out, g.come[2])
        pass_on(g, x, rows[3], to_down, g.out, g.come[3])
        pass_on(g, x, rows[2], to_up, g.out, g.near)
        pass_on(g, x, rows[3], to_up, g.out, g.near)
        pass_on(g, x, rows[1], to_down, g.out, g.near)
        g.given, g.give = mark(), sends(extent(g, pl.ds(0, nx), every))
        pass_on(g, x, every, sibling, g.give, g.given)

    def weights_on(g):
        block = extent(g, 0, 0)
        rows = [ahead(y, j, ny) for j in range(ny)]
        take(block, g.come[1])
        pass_on(g, down, rows[1], device(x=up), g.out, g.far)
        take(block, g.come[2])
        pass_on(g, up, rows[2], device(x=down), g.out, g.far)
        take(block, g.come[3])
        pass_on(g, up, rows[3], device(x=down), g.out, g.far)

    def weights_last(g):
        take(extent(g, 0, every), g.near)
        pass_on(g, down, every, sibling, g.give, g.given)
        pass_on(g, up, every, sibling, g.give, g.given)
        take(extent(g, 0, every), g.far)
        pass_on(g, ahead(x, 2, nx), every, sibling, g.give, g.given)

    for copy in small:
        copy.wait()
    for k in range(ns * ny):
        new_out[k] = new_ref[k]
    one, two = teams
    (a0, b0), (a1, b1) = one.parts, two.parts
    swap(one)
    swap(two)
    first_step(a0)
    first_step(b0)
    first_step(a1)
    first_step(b1)
    second_step(a0)
    second_step(b0)
    state_first()
    t = step_ref[0]
    fix_one = 1.0 - power(0.9, t)
    fix_two = 1.0 - power(0.95, t)
    second_step(a1)
    second_step(b1)
    third_step(a0)
    third_step(b0)
    state_second()
    third_step(a1)
    third_step(b1)
    sum_z(one)
    sum_z(two)
    state_done()
    update(one, fix_one, fix_two)
    update(two, fix_one, fix_two)
    weights_y(one)
    masters_z(one)
    pairs_own(one)
    weights_y(two)
    masters_z(two)
    pairs_own(two)
    weights_x(one)
    weights_x(two)
    pairs_y(one)
    weights_on(one)
    pairs_y(two)
    weights_on(two)
    weights_last(one)
    weights_last(two)
    for g in teams:
        pairs_done(g)
        take(extent(g, pl.ds(0, nx), every), g.given)
    finish()


def spread_kernel(dims, new_ref, gathered, pairs, master_out, first_out, second_out, weights_out, sem):
    nx, ny, nzh, _, _ = dims
    copies = []
    for a, ref in enumerate((master_out, first_out, second_out)):
        copies.append(pltpu.make_async_copy(pairs.at[a], ref, sem.at[1 + a]))
        copies[-1].start()
    for k in range(nzh * nx * ny):
        e, at_x, at_y = k // (nx * ny), k // ny % nx, k % ny
        copy = (
            pltpu.make_async_copy(gathered.at[(at_x * ny + at_y) * nzh + e], weights_out.at[new_ref[k]], sem.at[4])
        )
        copy.start()
    for copy in copies:
        copy.wait()
    pltpu.make_async_copy(gathered, gathered, sem.at[4]).wait()


def step_call(dims, groups, stop, old_order, new_order, step, grads, master, first, second):
    nx, ny, nzh, nzl, tiles = dims
    nz, ns, nb = nzh * nzl, nzh * nx, ny // 2
    half = tiles * LANES
    blocks = ns * ny
    vmem = pltpu.VMEM
    anywhere = pl.BlockSpec(memory_space=pl.ANY)
    scalars = pl.BlockSpec(memory_space=pltpu.SMEM)
    outside = pl.BlockSpec(memory_space=pltpu.HBM)
    inside = pl.BlockSpec(memory_space=pltpu.VMEM)
    buffers, state_width = [], 0
    for chunks in groups:
        for along_x, count_tiles in chunks:
            n1, n2 = (nx, ny) if along_x else (ny, nx)
            size = count_tiles * LANES
            buffers += [
                vmem((8 * blocks, size), BF16),
                vmem((8 * blocks, size), BF16),
                vmem((blocks, 8, size), F32),
                vmem((n1, n2, nzh, 8, size), F32),
                vmem((2, n2 // 2, nzh, 8, size), F32),
                vmem((min(n1 - 1, 2), n2, nzh, 8, size), F32),
                vmem((n2, nzh, 8, size), F32),
                vmem((n2 - 1, nzh, 8, size), F32),
            ]
        group_tiles = sum(n for _, n in chunks)
        size = group_tiles * LANES
        width = -(-group_tiles // nzl) * LANES
        fold = -(-width // (2 * LANES)) * LANES
        state_width += width
        buffers += [
            vmem((nzh, 8, size), F32),
            vmem((nz - 1, 8, width), F32),
            vmem((3, 8, width), F32),
            vmem((nzl, 3, 8, width), F32),
            vmem((16, fold), BF16),
            vmem((nz, 16, fold), BF16),
            vmem((8 * nzh, size), BF16),
            vmem((3, 8, size), F32),
        ]
    gathered, pairs, kept = pl.pallas_call(
        functools.partial(kernel, dims, groups, stop),
        out_shape=(pltpu.VMEM((nx, ny, 8 * nzh, 2 * half), BF16), pltpu.VMEM((3, nb, 8, 2 * half), F32), pltpu.SMEM((blocks,), jnp.int32)),
        in_specs=[anywhere] * 3 + [outside] * 4,
        out_specs=[inside] * 2 + [scalars],
        scratch_shapes=[
            pltpu.SMEM((blocks,), jnp.int32),
            pltpu.SMEM((blocks,), jnp.int32),
            pltpu.SMEM((1,), jnp.int32),
            vmem((3, ny, 8, state_width), F32),
            vmem((ns, 8, state_width), F32),
            vmem((ns, 8, state_width), F32),
            vmem((ny, 8, state_width), F32),
            vmem((3, 8, state_width), F32),
            pltpu.SemaphoreType.DMA((MARKS,)),
        ] + buffers,
        compiler_params=pltpu.CompilerParams(
            collective_id=0, has_side_effects=True, vmem_limit_bytes=60 * 1024 * 1024
        ),
        cost_estimate=pl.CostEstimate(flops=4_000_000, bytes_accessed=8_000_000, transcendentals=0),
    )(old_order, new_order, step, grads, master, first, second)
    f32_out = jax.ShapeDtypeStruct((nb, 8, 2 * half), F32)
    return pl.pallas_call(
        functools.partial(spread_kernel, dims),
        out_shape=(f32_out, f32_out, f32_out, jax.ShapeDtypeStruct((blocks, 8, 2 * half), BF16)),
        in_specs=[scalars, inside, inside],
        out_specs=[anywhere] * 4,
        scratch_shapes=[pltpu.SemaphoreType.DMA((5,))],
        compiler_params=pltpu.CompilerParams(vmem_limit_bytes=8 * 1024 * 1024),
    )(kept, gathered.reshape(blocks, 8, 2 * half), pairs)


def body(dims, groups, stop, master_old, moment_one_old, moment_two_old, grads, old_order, new_order, step):
    blocks, rows, columns = grads.shape[2:]
    flat = grads.reshape(blocks * rows, columns)
    master, first, second, weights = step_call(
        dims, groups, stop, old_order, new_order, step, flat, master_old, moment_one_old, moment_two_old
    )
    return master[None], first[None], second[None], weights[None]


GROUPS = (((True, 4), (False, 4)), ((True, 5), (False, 5)))


def solution(mesh, dims=(4, 4, 2, 4, 18), groups=GROUPS, stop=0):
    return jax.shard_map(
        functools.partial(body, dims, groups, stop),
        mesh=mesh,
        in_specs=(
            P("shard", None, None),
            P("shard", None, None),
            P("shard", None, None),
            P("rep", "shard", None, None, None),
            P(),
            P(),
            P(),
        ),
        out_specs=(
            P("rep", "shard", None, None),
            P("rep", "shard", None, None),
            P("rep", "shard", None, None),
            P("rep", None, None, None),
        ),
        check_vma=False,
    )
```

```python
import functools
from types import SimpleNamespace

import jax
import jax.numpy as jnp
import numpy as np
from jax import lax
from jax.experimental import pallas as pl
from jax.experimental.pallas import tpu as pltpu
from jax.sharding import PartitionSpec as P

MESH = pl.DeviceIdType.MESH
LANES = 128
MARKS = 97
F32 = jnp.float32
BF16 = jnp.bfloat16


def power(base, count):
    out = jnp.float32(1.0)
    for bit in range(11):
        factor = np.float32(float(base) ** (1 << bit))
        taken = lax.rem(lax.shift_right_logical(count, jnp.int32(bit)), jnp.int32(2)) == 1
        out = jnp.where(taken, out * factor, out)
    return jnp.where(count >= 2048, jnp.float32(0.0), out)


def kernel(
    dims, groups, stop,
    old_in, new_in, step_in, grads, master, first, second,
    gathered, pairs, new_out,
    old_ref, new_ref, step_ref,
    state, state_out, cand, turn, owned,
    sems, *buffers,
):
    nx, ny, nzh, nzl, tiles = dims
    nz, ns, nb = nzh * nzl, nzh * nx, ny // 2
    half = tiles * LANES

    rep, shard = lax.axis_index("rep"), lax.axis_index("shard")
    core = lax.rem(rep, 2)
    y = lax.rem(lax.div(rep, 2), ny)
    zl = lax.div(rep, 2 * ny)
    x, zh = lax.rem(shard, nx), lax.div(shard, nx)
    z = zh * nzl + zl

    def device(x=x, y=y, zh=zh, zl=zl, core=core):
        return ((zl * ny + y) * 2 + core, zh * nx + x)

    def on_x(to):
        return device(x=to)

    def on_y(to):
        return device(y=to)

    def ahead(value, by, size):
        return lax.rem(value + by, size)

    used = []
    ends = []

    def mark():
        used.append(1)
        return sems.at[len(used) - 1]

    def take(ref, sem):
        pltpu.make_async_copy(ref, ref, sem).wait()

    def remote(src, dst, to, send, recv, when=None):
        copy = pltpu.make_async_remote_copy(
            src_ref=src, dst_ref=dst, send_sem=send, recv_sem=recv, device_id=to, device_id_type=MESH
        )
        if when is None:
            copy.start()
        else:
            pl.when(when)(copy.start)

    def local(src, dst, sem):
        copy = pltpu.make_async_copy(src, dst, sem)
        copy.start()
        return copy

    def sends(ref, when=None):
        sem = mark()
        ends.append((ref, sem, when))
        return sem

    def finish():
        for ref, sem, when in ends:
            if when is None:
                take(ref, sem)
            else:
                pl.when(when)(functools.partial(take, ref, sem))

    far = lambda n: sorted(range(1, n), key=lambda d: -min(d, n - d))
    mine = pl.multiple_of(core * half, LANES)
    theirs = pl.multiple_of((1 - core) * half, LANES)
    sibling = device(core=1 - core)

    teams, column, k = [], 0, 0
    for chunks in groups:
        g = SimpleNamespace(at=column, parts=[], tiles=sum(n for _, n in chunks))
        inner = 0
        for along_x, count_tiles in chunks:
            p = SimpleNamespace(along_x=along_x, at=column + inner, inner=inner, size=count_tiles * LANES)
            p.own, p.sib, p.chip, p.send, p.relay, p.recv1, p.part, p.recv2 = buffers[k:k + 8]
            k += 8
            p.n1, p.n2, p.me1, p.me2 = (nx, ny, x, y) if along_x else (ny, nx, y, x)
            p.to1, p.to2 = (on_x, on_y) if along_x else (on_y, on_x)
            inner += count_tiles * LANES
            g.parts.append(p)
        g.sum, g.recv3, g.result, g.result_z, g.short, g.short_z, g.wide, g.pair = buffers[k:k + 8]
        k += 8
        g.size = inner
        g.width = g.result.shape[2]
        g.fold = g.short.shape[1]
        g.starts = [(q * g.tiles // nzl) * LANES for q in range(nzl + 1)]
        column += inner
        teams.append(g)

    def piece(g, q):
        return pl.multiple_of(lax.div(q * g.tiles, nzl) * LANES, LANES)

    small = [local(src, dst, mark()) for src, dst in ((old_in, old_ref), (new_in, new_ref), (step_in, step_ref))]
    for g in teams:
        for p in g.parts:
            p.load = local(grads.at[:, pl.ds(mine + p.at, p.size)], p.own, mark())
    state_mark, column = mark(), 0
    for g in teams:
        g.state_at = column
        for a, ref in enumerate((master, first, second)):
            spot = pl.ds(mine + g.at + piece(g, zl), g.width)
            local(ref.at[:, :, spot], state.at[a, :, :, pl.ds(column, g.width)], state_mark)
        column += g.width

    partners = [sibling]
    partners += [device(x=ahead(x, d, nx)) for d in range(1, nx)]
    for d in range(1, ny):
        partners += [device(y=ahead(y, d, ny)), device(y=ahead(y, d, ny), core=1 - core)]
    for d in range(1, nz):
        other = ahead(z, d, nz)
        partners.append(device(zh=lax.div(other, nzl), zl=lax.rem(other, nzl)))
    for e in range(1, nzh):
        partners += [device(x=ahead(x, d, nx), zh=ahead(zh, e, nzh)) for d in range(1, nx)]
    barrier = pltpu.get_barrier_semaphore()
    for partner in partners:
        pl.semaphore_signal(barrier, inc=1, device_id=partner, device_id_type=MESH)
    pl.semaphore_wait(barrier, len(partners))

    swap_send = sends(grads.at[:, pl.ds(0, half)])

    def swap(g):
        for p in g.parts:
            p.swap = mark()
            remote(grads.at[:, pl.ds(theirs + p.at, p.size)], p.sib, sibling, swap_send, p.swap)


    holds = y < 3
    kind = jnp.where(holds, y, 2)
    moved = state_out.at[pl.ds(1, ns - 1)]
    move_send, move_recv = sends(moved, holds), mark()
    turn_marks = [mark() for _ in range(3)]
    turn_send = mark()
    turn_recv = sems.at[kind + (len(used) - 4)]
    ends.append((turn.at[pl.ds(0, ny - 1)], turn_send, holds))

    def state_first():
        take(state, state_mark)
        for e in range(nzh - 1, -1, -1):
            for d in far(nx) + [0]:
                to_x, to_zh = ahead(x, d, nx), ahead(zh, e, nzh)
                to_slot = (to_zh * nx + to_x) * ny
                pick = jnp.int32(0)
                for j in range(1, ny):
                    block = old_ref[shard * ny + j]
                    for q in range(ny):
                        pick = jnp.where(new_ref[to_slot + q] == block, jnp.int32(j), pick)
                slot = e * nx + d
                target = state_out if slot else cand
                target[slot] = state[kind, pick]
                if slot:
                    to = device(x=to_x, zh=to_zh)
                    remote(state_out.at[slot], cand.at[slot], to, move_send, move_recv, holds)

    def state_second():
        picks = []
        for q in range(ny):
            wanted = new_ref[shard * ny + q]
            pick = jnp.int32(0)
            for e in range(nzh):
                for d in range(nx):
                    if e or d:
                        from_x, from_zh = ahead(x, nx - d, nx), ahead(zh, nzh - e, nzh)
                        for j in range(ny):
                            match = old_ref[(from_zh * nx + from_x) * ny + j] == wanted
                            pick = jnp.where(match, jnp.int32(e * nx + d), pick)
            picks.append(pick)
        pl.when(holds)(functools.partial(take, moved, move_recv))
        for q in range(ny):
            turn[q] = cand[picks[q]]
            away = jnp.logical_and(holds, y != q)
            remote(turn.at[q], owned.at[kind], device(y=q), turn_send, turn_recv, away)

        @pl.when(holds)
        def _():
            owned[kind] = turn[y]

    def state_done():
        for a in range(3):
            pl.when(y != a)(functools.partial(take, owned.at[a], turn_marks[a]))

    def chip_sum(p):
        p.load.wait()
        take(p.sib, p.swap)

        def add(i, carry):
            rows = pl.ds(pl.multiple_of(i * 16, 16), 16)
            both = p.own[rows, :].astype(F32) + p.sib[rows, :].astype(F32)
            p.chip[2 * i] = both[:8]
            p.chip[2 * i + 1] = both[8:]
            return carry

        lax.fori_loop(0, ns * ny // 2, add, 0)

    def order(p, lead):
        for inner in range(p.n2):
            for e in range(nzh):
                to_x, to_y = (lead, inner) if p.along_x else (inner, lead)
                p.send[lead, inner, e] = p.chip[new_ref[(e * nx + to_x) * ny + to_y]]

    def first_step(p):
        chip_sum(p)
        n, me, h = p.n1, p.me1, p.n2 // 2
        low, high = pl.ds(0, h), pl.ds(h, h)
        up, down = ahead(me, 1, n), ahead(me, n - 1, n)
        if n == 2:
            order(p, up)
            p.got = mark()
            remote(p.send.at[up], p.recv1.at[0], p.to1(up), sends(p.send.at[0]), p.got)
            order(p, me)
            return
        to_up, to_down = p.to1(up), p.to1(down)
        across = ahead(me, 2, n)
        order(p, across)
        p.relays, p.got, p.out = [mark(), mark()], mark(), sends(p.send.at[pl.ds(0, 3)])
        out, got = p.out, p.got
        remote(p.send.at[across, low], p.relay.at[0], to_up, out, p.relays[0])
        remote(p.send.at[across, high], p.relay.at[1], to_down, out, p.relays[1])
        order(p, up)
        remote(p.send.at[up, high], p.recv1.at[0, high], to_up, out, got)
        order(p, down)
        remote(p.send.at[down, low], p.recv1.at[1, low], to_down, out, got)
        order(p, me)

    def second_step(p):
        n, me, h = p.n1, p.me1, p.n2 // 2
        if n == 2:
            return
        low, high = pl.ds(0, h), pl.ds(h, h)
        up, down = ahead(me, 1, n), ahead(me, n - 1, n)
        to_up, to_down = p.to1(up), p.to1(down)
        take(p.relay.at[0], p.relays[0])
        p.send[up, low] = p.send[up, low] + p.relay[0]
        remote(p.send.at[up, low], p.recv1.at[0, low], to_up, p.out, p.got)
        take(p.relay.at[1], p.relays[1])
        p.send[down, high] = p.send[down, high] + p.relay[1]
        remote(p.send.at[down, high], p.recv1.at[1, high], to_down, p.out, p.got)

    def third_step(p):
        take(p.recv1, p.got)
        p.second, out = mark(), sends(p.recv2)
        for d in far(p.n2) + [0]:
            to = ahead(p.me2, d, p.n2)
            for e in range(nzh):
                total = p.send[p.me1, to, e]
                for q in range(min(p.n1 - 1, 2)):
                    total = total + p.recv1[q, to, e]
                p.part[to, e] = total
            if d:
                remote(p.part.at[to], p.recv2.at[d - 1], p.to2(to), out, p.second)

    def sum_z(g):
        for p in g.parts:
            take(p.recv2, p.second)
            for e in range(nzh):
                total = p.part[p.me2, e]
                for q in range(p.n2 - 1):
                    total = total + p.recv2[q, e]
                g.sum[e, :, p.inner:p.inner + p.size] = total
        g.third, out = mark(), sends(g.recv3)
        for d in far(nz):
            other = ahead(z, d, nz)
            to_zh, to_zl = lax.div(other, nzl), lax.rem(other, nzl)
            src = g.sum.at[to_zh, :, pl.ds(piece(g, to_zl), g.width)]
            remote(src, g.recv3.at[d - 1], device(zh=to_zh, zl=to_zl), out, g.third)

    def update(g, fix_one, fix_two):
        take(g.recv3, g.third)
        grad = g.sum[zh, :, pl.ds(piece(g, zl), g.width)]
        for q in range(nz - 1):
            grad = grad + g.recv3[q]
        spot = slice(g.state_at, g.state_at + g.width)
        weight = owned[0, :, spot]
        moment_one = 0.9 * owned[1, :, spot] + 0.1 * grad
        moment_two = 0.95 * owned[2, :, spot] + 0.05 * grad * grad
        direction = moment_one / fix_one / (jnp.sqrt(moment_two / fix_two) + 1e-08)
        updated = weight - 0.1 * (direction + 0.1 * weight)
        fold, short, short_z = g.fold, g.short, g.short_z
        rest = updated[:, fold:]
        if rest.shape[1] < fold:
            rest = jnp.concatenate([rest, jnp.zeros((8, fold - rest.shape[1]), F32)], axis=1)
        short[...] = jnp.concatenate([updated[:, :fold], rest], axis=0).astype(BF16)
        g.over_z, out = mark(), sends(short_z.at[pl.ds(0, nz - 1)])
        for d in far(nz):
            other = ahead(z, d, nz)
            to = device(zh=lax.div(other, nzl), zl=lax.rem(other, nzl))
            remote(short, short_z.at[z], to, out, g.over_z)
        short_z[z] = short[...]
        for a, value in enumerate((updated, moment_one, moment_two)):
            g.result[a] = value
            g.result_z[zl, a] = value

    every = pl.ds(0, ny)
    up, down = ahead(x, 1, nx), ahead(x, nx - 1, nx)

    def extent(g, of, rows):
        return gathered.at[of, rows, :, pl.ds(0, g.size)]

    def block_place(g, of_x, of_y):
        return gathered.at[of_x, of_y, :, pl.ds(mine + g.at, g.size)]

    def weights_y(g):
        take(g.short_z.at[pl.ds(0, nz - 1)], g.over_z)
        starts, fold = g.starts, g.fold
        for q in range(nzl):
            span = starts[q + 1] - starts[q]
            for low, high, top in ((0, min(span, fold), 0), (fold, span, 8)):
                if high > low:
                    rows = [g.short_z[e * nzl + q, :, :high - low].astype(F32)[top:top + 8] for e in range(nzh)]
                    g.wide[:, starts[q] + low:starts[q] + high] = jnp.concatenate(rows, axis=0).astype(BF16)
        place = block_place(g, x, y)
        g.over_y, out = mark(), sends(extent(g, 0, pl.ds(0, ny - 1)))
        g.out = sends(extent(g, pl.ds(0, 3), every))
        g.come, g.near, g.far = [mark() for _ in range(4)], mark(), mark()
        remote(g.wide, place, device(x=up), g.out, g.come[0])
        remote(g.wide, place, device(x=down), g.out, g.near)
        for d in far(ny):
            remote(g.wide, place, device(y=ahead(y, d, ny)), out, g.over_y)
        g.kept = local(g.wide, place, mark())

    def masters_z(g):
        g.over_zl = [mark() for _ in range(nzl)]
        landed = sems.at[len(used) - nzl + zl]
        if nzl > 1:
            out = sends(g.result_z.at[pl.ds(0, nzl - 1)])
        for d in far(nzl):
            remote(g.result, g.result_z.at[zl], device(zl=ahead(zl, d, nzl)), out, landed)

    member, row = lax.div(y, nb), lax.rem(y, nb)

    def hand_out(g, q, src, when):
        at, wide = g.starts[q], g.starts[q + 1] - g.starts[q]
        src = src.at[:, :, pl.ds(0, wide)]
        place = pairs.at[:, row, :, pl.ds(mine + g.at + at, wide)]
        for d in far(ny):
            remote(src, place, device(y=ahead(y, d, ny), core=member), g.pair_out, g.landed, when)
        remote(src, place, sibling, g.pair_give, g.landed, jnp.logical_and(when, member != core))
        within = pltpu.make_async_copy(src, place, g.landed)
        pl.when(jnp.logical_and(when, member == core))(within.start)

    def pairs_own(g):
        g.pair_marks = [mark() for _ in range(2 * nb)]
        g.landed = sems.at[len(used) - 2 * nb + row * 2 + core]
        g.pair_out = sends(pairs.at[:, 0, :, pl.ds(0, (ny - 1) * g.size)])
        g.pair_give = sends(g.pair, member != core)
        for q in range(nzl):
            hand_out(g, q, g.result, zl == q)

    def pairs_y(g):
        for q in range(nzl):
            pl.when(zl != q)(functools.partial(take, g.result_z.at[q], g.over_zl[q]))
            hand_out(g, q, g.result_z.at[q], zl != q)

    def pairs_done(g):
        for k in range(2 * nb):
            take(g.pair, g.pair_marks[k])

    def pass_on(g, of, rows, to, send, recv):
        place = gathered.at[of, rows, :, pl.ds(mine + g.at, g.size)]
        remote(place, place, to, send, recv)

    def weights_x(g):
        to_up, to_down = device(x=up), device(x=down)
        block = extent(g, 0, 0)
        rows = [ahead(y, j, ny) for j in range(ny)]
        take(block, g.come[0])
        pass_on(g, down, rows[0], to_up, g.out, g.far)
        take(extent(g, 0, pl.ds(0, ny - 1)), g.over_y)
        g.kept.wait()
        pass_on(g, x, rows[1], to_up, g.out, g.come[1])
        pass_on(g, x, rows[2], to_down, g.out, g.come[2])
        pass_on(g, x, rows[3], to_down, g.out, g.come[3])
        pass_on(g, x, rows[2], to_up, g.out, g.near)
        pass_on(g, x, rows[3], to_up, g.out, g.near)
        pass_on(g, x, rows[1], to_down, g.out, g.near)
        g.given, g.give = mark(), sends(extent(g, pl.ds(0, nx), every))
        pass_on(g, x, every, sibling, g.give, g.given)

    def weights_on(g):
        block = extent(g, 0, 0)
        rows = [ahead(y, j, ny) for j in range(ny)]
        take(block, g.come[1])
        pass_on(g, down, rows[1], device(x=up), g.out, g.far)
        take(block, g.come[2])
        pass_on(g, up, rows[2], device(x=down), g.out, g.far)
        take(block, g.come[3])
        pass_on(g, up, rows[3], device(x=down), g.out, g.far)

    def weights_last(g):
        take(extent(g, 0, every), g.near)
        pass_on(g, down, every, sibling, g.give, g.given)
        pass_on(g, up, every, sibling, g.give, g.given)
        take(extent(g, 0, every), g.far)
        pass_on(g, ahead(x, 2, nx), every, sibling, g.give, g.given)

    for copy in small:
        copy.wait()
    for k in range(ns * ny):
        new_out[k] = new_ref[k]
    one, two = teams
    (a0, b0), (a1, b1) = one.parts, two.parts
    swap(one)
    swap(two)
    state_first()
    first_step(a0)
    first_step(b0)
    first_step(a1)
    first_step(b1)
    second_step(a0)
    second_step(b0)
    t = step_ref[0]
    fix_one = 1.0 - power(0.9, t)
    fix_two = 1.0 - power(0.95, t)
    second_step(a1)
    second_step(b1)
    state_second()
    third_step(a0)
    third_step(b0)
    third_step(a1)
    third_step(b1)
    sum_z(one)
    sum_z(two)
    state_done()
    update(one, fix_one, fix_two)
    update(two, fix_one, fix_two)
    weights_y(one)
    pairs_own(one)
    masters_z(one)
    weights_y(two)
    pairs_own(two)
    masters_z(two)
    weights_x(one)
    weights_x(two)
    pairs_y(one)
    weights_on(one)
    pairs_y(two)
    weights_on(two)
    weights_last(one)
    weights_last(two)
    for g in teams:
        pairs_done(g)
        take(extent(g, pl.ds(0, nx), every), g.given)
    finish()


def spread_kernel(dims, new_ref, gathered, pairs, master_out, first_out, second_out, weights_out, sem):
    nx, ny, nzh, _, _ = dims
    copies = []
    for a, ref in enumerate((master_out, first_out, second_out)):
        copies.append(pltpu.make_async_copy(pairs.at[a], ref, sem.at[1 + a]))
        copies[-1].start()
    for k in range(nzh * nx * ny):
        e, at_x, at_y = k // (nx * ny), k // ny % nx, k % ny
        copy = (
            pltpu.make_async_copy(gathered.at[(at_x * ny + at_y) * nzh + e], weights_out.at[new_ref[k]], sem.at[4])
        )
        copy.start()
    for copy in copies:
        copy.wait()
    pltpu.make_async_copy(gathered, gathered, sem.at[4]).wait()


def step_call(dims, groups, stop, old_order, new_order, step, grads, master, first, second):
    nx, ny, nzh, nzl, tiles = dims
    nz, ns, nb = nzh * nzl, nzh * nx, ny // 2
    half = tiles * LANES
    blocks = ns * ny
    vmem = pltpu.VMEM
    anywhere = pl.BlockSpec(memory_space=pl.ANY)
    scalars = pl.BlockSpec(memory_space=pltpu.SMEM)
    outside = pl.BlockSpec(memory_space=pltpu.HBM)
    inside = pl.BlockSpec(memory_space=pltpu.VMEM)
    buffers, state_width = [], 0
    for chunks in groups:
        for along_x, count_tiles in chunks:
            n1, n2 = (nx, ny) if along_x else (ny, nx)
            size = count_tiles * LANES
            buffers += [
                vmem((8 * blocks, size), BF16),
                vmem((8 * blocks, size), BF16),
                vmem((blocks, 8, size), F32),
                vmem((n1, n2, nzh, 8, size), F32),
                vmem((2, n2 // 2, nzh, 8, size), F32),
                vmem((min(n1 - 1, 2), n2, nzh, 8, size), F32),
                vmem((n2, nzh, 8, size), F32),
                vmem((n2 - 1, nzh, 8, size), F32),
            ]
        group_tiles = sum(n for _, n in chunks)
        size = group_tiles * LANES
        width = -(-group_tiles // nzl) * LANES
        fold = -(-width // (2 * LANES)) * LANES
        state_width += width
        buffers += [
            vmem((nzh, 8, size), F32),
            vmem((nz - 1, 8, width), F32),
            vmem((3, 8, width), F32),
            vmem((nzl, 3, 8, width), F32),
            vmem((16, fold), BF16),
            vmem((nz, 16, fold), BF16),
            vmem((8 * nzh, size), BF16),
            vmem((3, 8, size), F32),
        ]
    gathered, pairs, kept = pl.pallas_call(
        functools.partial(kernel, dims, groups, stop),
        out_shape=(pltpu.VMEM((nx, ny, 8 * nzh, 2 * half), BF16), pltpu.VMEM((3, nb, 8, 2 * half), F32), pltpu.SMEM((blocks,), jnp.int32)),
        in_specs=[anywhere] * 3 + [outside] * 4,
        out_specs=[inside] * 2 + [scalars],
        scratch_shapes=[
            pltpu.SMEM((blocks,), jnp.int32),
            pltpu.SMEM((blocks,), jnp.int32),
            pltpu.SMEM((1,), jnp.int32),
            vmem((3, ny, 8, state_width), F32),
            vmem((ns, 8, state_width), F32),
            vmem((ns, 8, state_width), F32),
            vmem((ny, 8, state_width), F32),
            vmem((3, 8, state_width), F32),
            pltpu.SemaphoreType.DMA((MARKS,)),
        ] + buffers,
        compiler_params=pltpu.CompilerParams(
            collective_id=0, has_side_effects=True, vmem_limit_bytes=60 * 1024 * 1024
        ),
        cost_estimate=pl.CostEstimate(flops=4_000_000, bytes_accessed=8_000_000, transcendentals=0),
    )(old_order, new_order, step, grads, master, first, second)
    f32_out = jax.ShapeDtypeStruct((nb, 8, 2 * half), F32)
    return pl.pallas_call(
        functools.partial(spread_kernel, dims),
        out_shape=(f32_out, f32_out, f32_out, jax.ShapeDtypeStruct((blocks, 8, 2 * half), BF16)),
        in_specs=[scalars, inside, inside],
        out_specs=[anywhere] * 4,
        scratch_shapes=[pltpu.SemaphoreType.DMA((5,))],
        compiler_params=pltpu.CompilerParams(vmem_limit_bytes=8 * 1024 * 1024),
    )(kept, gathered.reshape(blocks, 8, 2 * half), pairs)


def body(dims, groups, stop, master_old, moment_one_old, moment_two_old, grads, old_order, new_order, step):
    blocks, rows, columns = grads.shape[2:]
    flat = grads.reshape(blocks * rows, columns)
    master, first, second, weights = step_call(
        dims, groups, stop, old_order, new_order, step, flat, master_old, moment_one_old, moment_two_old
    )
    return master[None], first[None], second[None], weights[None]


GROUPS = (((True, 4), (False, 4)), ((True, 5), (False, 5)))


def solution(mesh, dims=(4, 4, 2, 4, 18), groups=GROUPS, stop=0):
    return jax.shard_map(
        functools.partial(body, dims, groups, stop),
        mesh=mesh,
        in_specs=(
            P("shard", None, None),
            P("shard", None, None),
            P("shard", None, None),
            P("rep", "shard", None, None, None),
            P(),
            P(),
            P(),
        ),
        out_specs=(
            P("rep", "shard", None, None),
            P("rep", "shard", None, None),
            P("rep", "shard", None, None),
            P("rep", None, None, None),
        ),
        check_vma=False,
    )
```

```python
import functools
from types import SimpleNamespace

import jax
import jax.numpy as jnp
import numpy as np
from jax import lax
from jax.experimental import pallas as pl
from jax.experimental.pallas import tpu as pltpu
from jax.sharding import PartitionSpec as P

MESH = pl.DeviceIdType.MESH
LANES = 128
MARKS = 97
F32 = jnp.float32
BF16 = jnp.bfloat16


def power(base, count):
    out = jnp.float32(1.0)
    for bit in range(11):
        factor = np.float32(float(base) ** (1 << bit))
        taken = lax.rem(lax.shift_right_logical(count, jnp.int32(bit)), jnp.int32(2)) == 1
        out = jnp.where(taken, out * factor, out)
    return jnp.where(count >= 2048, jnp.float32(0.0), out)


def kernel(
    dims, groups, stop,
    old_in, new_in, step_in, grads, master, first, second,
    gathered, pairs, new_out,
    old_ref, new_ref, step_ref,
    state, state_out, cand, turn, owned,
    sems, *buffers,
):
    nx, ny, nzh, nzl, tiles = dims
    nz, ns, nb = nzh * nzl, nzh * nx, ny // 2
    half = tiles * LANES

    rep, shard = lax.axis_index("rep"), lax.axis_index("shard")
    core = lax.rem(rep, 2)
    y = lax.rem(lax.div(rep, 2), ny)
    zl = lax.div(rep, 2 * ny)
    x, zh = lax.rem(shard, nx), lax.div(shard, nx)
    z = zh * nzl + zl

    def device(x=x, y=y, zh=zh, zl=zl, core=core):
        return ((zl * ny + y) * 2 + core, zh * nx + x)

    def on_x(to):
        return device(x=to)

    def on_y(to):
        return device(y=to)

    def ahead(value, by, size):
        return lax.rem(value + by, size)

    used = []
    ends = []

    def mark():
        used.append(1)
        return sems.at[len(used) - 1]

    def take(ref, sem):
        pltpu.make_async_copy(ref, ref, sem).wait()

    def remote(src, dst, to, send, recv, when=None):
        copy = pltpu.make_async_remote_copy(
            src_ref=src, dst_ref=dst, send_sem=send, recv_sem=recv, device_id=to, device_id_type=MESH
        )
        if when is None:
            copy.start()
        else:
            pl.when(when)(copy.start)

    def local(src, dst, sem):
        copy = pltpu.make_async_copy(src, dst, sem)
        copy.start()
        return copy

    def sends(ref, when=None):
        sem = mark()
        ends.append((ref, sem, when))
        return sem

    def finish():
        for ref, sem, when in ends:
            if when is None:
                take(ref, sem)
            else:
                pl.when(when)(functools.partial(take, ref, sem))

    far = lambda n: sorted(range(1, n), key=lambda d: -min(d, n - d))
    mine = pl.multiple_of(core * half, LANES)
    theirs = pl.multiple_of((1 - core) * half, LANES)
    sibling = device(core=1 - core)

    teams, column, k = [], 0, 0
    for chunks in groups:
        g = SimpleNamespace(at=column, parts=[], tiles=sum(n for _, n in chunks))
        inner = 0
        for along_x, count_tiles in chunks:
            p = SimpleNamespace(along_x=along_x, at=column + inner, inner=inner, size=count_tiles * LANES)
            p.own, p.sib, p.chip, p.send, p.relay, p.recv1, p.part, p.recv2 = buffers[k:k + 8]
            k += 8
            p.n1, p.n2, p.me1, p.me2 = (nx, ny, x, y) if along_x else (ny, nx, y, x)
            p.to1, p.to2 = (on_x, on_y) if along_x else (on_y, on_x)
            inner += count_tiles * LANES
            g.parts.append(p)
        g.sum, g.recv3, g.result, g.result_z, g.short, g.short_z, g.wide, g.pair = buffers[k:k + 8]
        k += 8
        g.size = inner
        g.width = g.result.shape[2]
        g.fold = g.short.shape[1]
        g.starts = [(q * g.tiles // nzl) * LANES for q in range(nzl + 1)]
        column += inner
        teams.append(g)

    def piece(g, q):
        return pl.multiple_of(lax.div(q * g.tiles, nzl) * LANES, LANES)

    small = [local(src, dst, mark()) for src, dst in ((old_in, old_ref), (new_in, new_ref), (step_in, step_ref))]
    for g in teams:
        for p in g.parts:
            p.load = local(grads.at[:, pl.ds(mine + p.at, p.size)], p.own, mark())
    state_mark, column = mark(), 0
    for g in teams:
        g.state_at = column
        for a, ref in enumerate((master, first, second)):
            spot = pl.ds(mine + g.at + piece(g, zl), g.width)
            local(ref.at[:, :, spot], state.at[a, :, :, pl.ds(column, g.width)], state_mark)
        column += g.width

    partners = [sibling]
    partners += [device(x=ahead(x, d, nx)) for d in range(1, nx)]
    for d in range(1, ny):
        partners += [device(y=ahead(y, d, ny)), device(y=ahead(y, d, ny), core=1 - core)]
    for d in range(1, nz):
        other = ahead(z, d, nz)
        partners.append(device(zh=lax.div(other, nzl), zl=lax.rem(other, nzl)))
    for e in range(1, nzh):
        partners += [device(x=ahead(x, d, nx), zh=ahead(zh, e, nzh)) for d in range(1, nx)]
    barrier = pltpu.get_barrier_semaphore()
    for partner in partners:
        pl.semaphore_signal(barrier, inc=1, device_id=partner, device_id_type=MESH)
    pl.semaphore_wait(barrier, len(partners))

    swap_send = sends(grads.at[:, pl.ds(0, half)])

    def swap(g):
        for p in g.parts:
            p.swap = mark()
            remote(grads.at[:, pl.ds(theirs + p.at, p.size)], p.sib, sibling, swap_send, p.swap)


    holds = y < 3
    kind = jnp.where(holds, y, 2)
    moved = state_out.at[pl.ds(1, ns - 1)]
    move_send, move_recv = sends(moved, holds), mark()
    turn_marks = [mark() for _ in range(3)]
    turn_send = mark()
    turn_recv = sems.at[kind + (len(used) - 4)]
    ends.append((turn.at[pl.ds(0, ny - 1)], turn_send, holds))

    def state_first():
        take(state, state_mark)
        for e in range(nzh - 1, -1, -1):
            for d in far(nx) + [0]:
                to_x, to_zh = ahead(x, d, nx), ahead(zh, e, nzh)
                to_slot = (to_zh * nx + to_x) * ny
                pick = jnp.int32(0)
                for j in range(1, ny):
                    block = old_ref[shard * ny + j]
                    for q in range(ny):
                        pick = jnp.where(new_ref[to_slot + q] == block, jnp.int32(j), pick)
                slot = e * nx + d
                target = state_out if slot else cand
                target[slot] = state[kind, pick]
                if slot:
                    to = device(x=to_x, zh=to_zh)
                    remote(state_out.at[slot], cand.at[slot], to, move_send, move_recv, holds)

    def state_second():
        picks = []
        for q in range(ny):
            wanted = new_ref[shard * ny + q]
            pick = jnp.int32(0)
            for e in range(nzh):
                for d in range(nx):
                    if e or d:
                        from_x, from_zh = ahead(x, nx - d, nx), ahead(zh, nzh - e, nzh)
                        for j in range(ny):
                            match = old_ref[(from_zh * nx + from_x) * ny + j] == wanted
                            pick = jnp.where(match, jnp.int32(e * nx + d), pick)
            picks.append(pick)
        pl.when(holds)(functools.partial(take, moved, move_recv))
        for q in range(ny):
            turn[q] = cand[picks[q]]
            away = jnp.logical_and(holds, y != q)
            remote(turn.at[q], owned.at[kind], device(y=q), turn_send, turn_recv, away)

        @pl.when(holds)
        def _():
            owned[kind] = turn[y]

    def state_done():
        for a in range(3):
            pl.when(y != a)(functools.partial(take, owned.at[a], turn_marks[a]))

    def chip_sum(p):
        p.load.wait()
        take(p.sib, p.swap)

        def add(i, carry):
            rows = pl.ds(pl.multiple_of(i * 16, 16), 16)
            both = p.own[rows, :].astype(F32) + p.sib[rows, :].astype(F32)
            p.chip[2 * i] = both[:8]
            p.chip[2 * i + 1] = both[8:]
            return carry

        lax.fori_loop(0, ns * ny // 2, add, 0, unroll=4)

    def order(p, lead):
        for inner in range(p.n2):
            for e in range(nzh):
                to_x, to_y = (lead, inner) if p.along_x else (inner, lead)
                p.send[lead, inner, e] = p.chip[new_ref[(e * nx + to_x) * ny + to_y]]

    def first_step(p):
        chip_sum(p)
        n, me, h = p.n1, p.me1, p.n2 // 2
        low, high = pl.ds(0, h), pl.ds(h, h)
        up, down = ahead(me, 1, n), ahead(me, n - 1, n)
        if n == 2:
            order(p, up)
            p.got = mark()
            remote(p.send.at[up], p.recv1.at[0], p.to1(up), sends(p.send.at[0]), p.got)
            order(p, me)
            return
        to_up, to_down = p.to1(up), p.to1(down)
        across = ahead(me, 2, n)
        order(p, across)
        p.relays, p.got, p.out = [mark(), mark()], mark(), sends(p.send.at[pl.ds(0, 3)])
        out, got = p.out, p.got
        remote(p.send.at[across, low], p.relay.at[0], to_up, out, p.relays[0])
        remote(p.send.at[across, high], p.relay.at[1], to_down, out, p.relays[1])
        order(p, up)
        remote(p.send.at[up, high], p.recv1.at[0, high], to_up, out, got)
        order(p, down)
        remote(p.send.at[down, low], p.recv1.at[1, low], to_down, out, got)
        order(p, me)

    def second_step(p):
        n, me, h = p.n1, p.me1, p.n2 // 2
        if n == 2:
            return
        low, high = pl.ds(0, h), pl.ds(h, h)
        up, down = ahead(me, 1, n), ahead(me, n - 1, n)
        to_up, to_down = p.to1(up), p.to1(down)
        take(p.relay.at[0], p.relays[0])
        p.send[up, low] = p.send[up, low] + p.relay[0]
        remote(p.send.at[up, low], p.recv1.at[0, low], to_up, p.out, p.got)
        take(p.relay.at[1], p.relays[1])
        p.send[down, high] = p.send[down, high] + p.relay[1]
        remote(p.send.at[down, high], p.recv1.at[1, high], to_down, p.out, p.got)

    def third_step(p):
        take(p.recv1, p.got)
        p.second, out = mark(), sends(p.recv2)
        for d in far(p.n2) + [0]:
            to = ahead(p.me2, d, p.n2)
            for e in range(nzh):
                total = p.send[p.me1, to, e]
                for q in range(min(p.n1 - 1, 2)):
                    total = total + p.recv1[q, to, e]
                p.part[to, e] = total
            if d:
                remote(p.part.at[to], p.recv2.at[d - 1], p.to2(to), out, p.second)

    def sum_z(g):
        for p in g.parts:
            take(p.recv2, p.second)
            for e in range(nzh):
                total = p.part[p.me2, e]
                for q in range(p.n2 - 1):
                    total = total + p.recv2[q, e]
                g.sum[e, :, p.inner:p.inner + p.size] = total
        g.third, out = mark(), sends(g.recv3)
        for d in far(nz):
            other = ahead(z, d, nz)
            to_zh, to_zl = lax.div(other, nzl), lax.rem(other, nzl)
            src = g.sum.at[to_zh, :, pl.ds(piece(g, to_zl), g.width)]
            remote(src, g.recv3.at[d - 1], device(zh=to_zh, zl=to_zl), out, g.third)

    def update(g, fix_one, fix_two):
        take(g.recv3, g.third)
        grad = g.sum[zh, :, pl.ds(piece(g, zl), g.width)]
        for q in range(nz - 1):
            grad = grad + g.recv3[q]
        spot = slice(g.state_at, g.state_at + g.width)
        weight = owned[0, :, spot]
        moment_one = 0.9 * owned[1, :, spot] + 0.1 * grad
        moment_two = 0.95 * owned[2, :, spot] + 0.05 * grad * grad
        direction = moment_one / fix_one / (jnp.sqrt(moment_two / fix_two) + 1e-08)
        updated = weight - 0.1 * (direction + 0.1 * weight)
        fold, short, short_z = g.fold, g.short, g.short_z
        rest = updated[:, fold:]
        if rest.shape[1] < fold:
            rest = jnp.concatenate([rest, jnp.zeros((8, fold - rest.shape[1]), F32)], axis=1)
        short[...] = jnp.concatenate([updated[:, :fold], rest], axis=0).astype(BF16)
        g.over_z, out = mark(), sends(short_z.at[pl.ds(0, nz - 1)])
        for d in far(nz):
            other = ahead(z, d, nz)
            to = device(zh=lax.div(other, nzl), zl=lax.rem(other, nzl))
            remote(short, short_z.at[z], to, out, g.over_z)
        short_z[z] = short[...]
        for a, value in enumerate((updated, moment_one, moment_two)):
            g.result[a] = value
            g.result_z[zl, a] = value

    every = pl.ds(0, ny)
    up, down = ahead(x, 1, nx), ahead(x, nx - 1, nx)

    def extent(g, of, rows):
        return gathered.at[of, rows, :, pl.ds(0, g.size)]

    def block_place(g, of_x, of_y):
        return gathered.at[of_x, of_y, :, pl.ds(mine + g.at, g.size)]

    def weights_y(g):
        take(g.short_z.at[pl.ds(0, nz - 1)], g.over_z)
        starts, fold = g.starts, g.fold
        for q in range(nzl):
            span = starts[q + 1] - starts[q]
            for low, high, top in ((0, min(span, fold), 0), (fold, span, 8)):
                if high > low:
                    rows = [g.short_z[e * nzl + q, :, :high - low].astype(F32)[top:top + 8] for e in range(nzh)]
                    g.wide[:, starts[q] + low:starts[q] + high] = jnp.concatenate(rows, axis=0).astype(BF16)
        place = block_place(g, x, y)
        g.over_y, out = mark(), sends(extent(g, 0, pl.ds(0, ny - 1)))
        g.out = sends(extent(g, pl.ds(0, 3), every))
        g.come, g.near, g.far = [mark() for _ in range(4)], mark(), mark()
        for d in far(ny):
            remote(g.wide, place, device(y=ahead(y, d, ny)), out, g.over_y)
        remote(g.wide, place, device(x=up), g.out, g.come[0])
        remote(g.wide, place, device(x=down), g.out, g.near)
        g.kept = local(g.wide, place, mark())

    def masters_z(g):
        g.over_zl = [mark() for _ in range(nzl)]
        landed = sems.at[len(used) - nzl + zl]
        if nzl > 1:
            out = sends(g.result_z.at[pl.ds(0, nzl - 1)])
        for d in far(nzl):
            remote(g.result, g.result_z.at[zl], device(zl=ahead(zl, d, nzl)), out, landed)

    member, row = lax.div(y, nb), lax.rem(y, nb)

    def hand_out(g, q, src, when):
        at, wide = g.starts[q], g.starts[q + 1] - g.starts[q]
        src = src.at[:, :, pl.ds(0, wide)]
        place = pairs.at[:, row, :, pl.ds(mine + g.at + at, wide)]
        for d in far(ny):
            remote(src, place, device(y=ahead(y, d, ny), core=member), g.pair_out, g.landed, when)
        remote(src, place, sibling, g.pair_give, g.landed, jnp.logical_and(when, member != core))
        within = pltpu.make_async_copy(src, place, g.landed)
        pl.when(jnp.logical_and(when, member == core))(within.start)

    def pairs_own(g):
        g.pair_marks = [mark() for _ in range(2 * nb)]
        g.landed = sems.at[len(used) - 2 * nb + row * 2 + core]
        g.pair_out = sends(pairs.at[:, 0, :, pl.ds(0, (ny - 1) * g.size)])
        g.pair_give = sends(g.pair, member != core)
        for q in range(nzl):
            hand_out(g, q, g.result, zl == q)

    def pairs_y(g):
        for q in range(nzl):
            pl.when(zl != q)(functools.partial(take, g.result_z.at[q], g.over_zl[q]))
            hand_out(g, q, g.result_z.at[q], zl != q)

    def pairs_done(g):
        for k in range(2 * nb):
            take(g.pair, g.pair_marks[k])

    def pass_on(g, of, rows, to, send, recv):
        place = gathered.at[of, rows, :, pl.ds(mine + g.at, g.size)]
        remote(place, place, to, send, recv)

    def weights_x(g):
        to_up, to_down = device(x=up), device(x=down)
        block = extent(g, 0, 0)
        rows = [ahead(y, j, ny) for j in range(ny)]
        take(extent(g, 0, pl.ds(0, ny - 1)), g.over_y)
        g.kept.wait()
        pass_on(g, x, rows[1], to_up, g.out, g.come[1])
        pass_on(g, x, rows[2], to_down, g.out, g.come[2])
        pass_on(g, x, rows[3], to_down, g.out, g.come[3])
        pass_on(g, x, rows[2], to_up, g.out, g.near)
        pass_on(g, x, rows[3], to_up, g.out, g.near)
        pass_on(g, x, rows[1], to_down, g.out, g.near)
        g.given, g.give = mark(), sends(extent(g, pl.ds(0, nx), every))
        pass_on(g, x, every, sibling, g.give, g.given)

    def weights_on(g):
        block = extent(g, 0, 0)
        rows = [ahead(y, j, ny) for j in range(ny)]
        take(block, g.come[0])
        pass_on(g, down, rows[0], device(x=up), g.out, g.far)
        take(block, g.come[1])
        pass_on(g, down, rows[1], device(x=up), g.out, g.far)
        take(block, g.come[2])
        pass_on(g, up, rows[2], device(x=down), g.out, g.far)
        take(block, g.come[3])
        pass_on(g, up, rows[3], device(x=down), g.out, g.far)

    def weights_last(g):
        take(extent(g, 0, every), g.near)
        pass_on(g, down, every, sibling, g.give, g.given)
        pass_on(g, up, every, sibling, g.give, g.given)
        take(extent(g, 0, every), g.far)
        pass_on(g, ahead(x, 2, nx), every, sibling, g.give, g.given)

    for copy in small:
        copy.wait()
    for k in range(ns * ny):
        new_out[k] = new_ref[k]
    one, two = teams
    (a0, b0), (a1, b1) = one.parts, two.parts
    swap(one)
    swap(two)
    state_first()
    first_step(a0)
    first_step(b0)
    first_step(a1)
    first_step(b1)
    second_step(a0)
    second_step(b0)
    t = step_ref[0]
    fix_one = 1.0 - power(0.9, t)
    fix_two = 1.0 - power(0.95, t)
    second_step(a1)
    second_step(b1)
    state_second()
    third_step(a0)
    third_step(b0)
    third_step(a1)
    third_step(b1)
    sum_z(one)
    sum_z(two)
    state_done()
    update(one, fix_one, fix_two)
    update(two, fix_one, fix_two)
    weights_y(one)
    pairs_own(one)
    masters_z(one)
    weights_y(two)
    pairs_own(two)
    masters_z(two)
    weights_x(one)
    weights_x(two)
    pairs_y(one)
    weights_on(one)
    pairs_y(two)
    weights_on(two)
    weights_last(one)
    weights_last(two)
    for g in teams:
        pairs_done(g)
        take(extent(g, pl.ds(0, nx), every), g.given)
    finish()


def spread_kernel(dims, new_ref, gathered, pairs, master_out, first_out, second_out, weights_out, sem):
    nx, ny, nzh, _, _ = dims
    copies = []
    for a, ref in enumerate((master_out, first_out, second_out)):
        copies.append(pltpu.make_async_copy(pairs.at[a], ref, sem.at[1 + a]))
        copies[-1].start()
    for k in range(nzh * nx * ny):
        e, at_x, at_y = k // (nx * ny), k // ny % nx, k % ny
        copy = (
            pltpu.make_async_copy(gathered.at[(at_x * ny + at_y) * nzh + e], weights_out.at[new_ref[k]], sem.at[4])
        )
        copy.start()
    for copy in copies:
        copy.wait()
    pltpu.make_async_copy(gathered, gathered, sem.at[4]).wait()


def step_call(dims, groups, stop, old_order, new_order, step, grads, master, first, second):
    nx, ny, nzh, nzl, tiles = dims
    nz, ns, nb = nzh * nzl, nzh * nx, ny // 2
    half = tiles * LANES
    blocks = ns * ny
    vmem = pltpu.VMEM
    anywhere = pl.BlockSpec(memory_space=pl.ANY)
    scalars = pl.BlockSpec(memory_space=pltpu.SMEM)
    outside = pl.BlockSpec(memory_space=pltpu.HBM)
    inside = pl.BlockSpec(memory_space=pltpu.VMEM)
    buffers, state_width = [], 0
    for chunks in groups:
        for along_x, count_tiles in chunks:
            n1, n2 = (nx, ny) if along_x else (ny, nx)
            size = count_tiles * LANES
            buffers += [
                vmem((8 * blocks, size), BF16),
                vmem((8 * blocks, size), BF16),
                vmem((blocks, 8, size), F32),
                vmem((n1, n2, nzh, 8, size), F32),
                vmem((2, n2 // 2, nzh, 8, size), F32),
                vmem((min(n1 - 1, 2), n2, nzh, 8, size), F32),
                vmem((n2, nzh, 8, size), F32),
                vmem((n2 - 1, nzh, 8, size), F32),
            ]
        group_tiles = sum(n for _, n in chunks)
        size = group_tiles * LANES
        width = -(-group_tiles // nzl) * LANES
        fold = -(-width // (2 * LANES)) * LANES
        state_width += width
        buffers += [
            vmem((nzh, 8, size), F32),
            vmem((nz - 1, 8, width), F32),
            vmem((3, 8, width), F32),
            vmem((nzl, 3, 8, width), F32),
            vmem((16, fold), BF16),
            vmem((nz, 16, fold), BF16),
            vmem((8 * nzh, size), BF16),
            vmem((3, 8, size), F32),
        ]
    gathered, pairs, kept = pl.pallas_call(
        functools.partial(kernel, dims, groups, stop),
        out_shape=(pltpu.VMEM((nx, ny, 8 * nzh, 2 * half), BF16), pltpu.VMEM((3, nb, 8, 2 * half), F32), pltpu.SMEM((blocks,), jnp.int32)),
        in_specs=[anywhere] * 3 + [outside] * 4,
        out_specs=[inside] * 2 + [scalars],
        scratch_shapes=[
            pltpu.SMEM((blocks,), jnp.int32),
            pltpu.SMEM((blocks,), jnp.int32),
            pltpu.SMEM((1,), jnp.int32),
            vmem((3, ny, 8, state_width), F32),
            vmem((ns, 8, state_width), F32),
            vmem((ns, 8, state_width), F32),
            vmem((ny, 8, state_width), F32),
            vmem((3, 8, state_width), F32),
            pltpu.SemaphoreType.DMA((MARKS,)),
        ] + buffers,
        compiler_params=pltpu.CompilerParams(
            collective_id=0, has_side_effects=True, vmem_limit_bytes=60 * 1024 * 1024
        ),
        cost_estimate=pl.CostEstimate(flops=4_000_000, bytes_accessed=8_000_000, transcendentals=0),
    )(old_order, new_order, step, grads, master, first, second)
    f32_out = jax.ShapeDtypeStruct((nb, 8, 2 * half), F32)
    return pl.pallas_call(
        functools.partial(spread_kernel, dims),
        out_shape=(f32_out, f32_out, f32_out, jax.ShapeDtypeStruct((blocks, 8, 2 * half), BF16)),
        in_specs=[scalars, inside, inside],
        out_specs=[anywhere] * 4,
        scratch_shapes=[pltpu.SemaphoreType.DMA((5,))],
        compiler_params=pltpu.CompilerParams(vmem_limit_bytes=8 * 1024 * 1024),
    )(kept, gathered.reshape(blocks, 8, 2 * half), pairs)


def body(dims, groups, stop, master_old, moment_one_old, moment_two_old, grads, old_order, new_order, step):
    blocks, rows, columns = grads.shape[2:]
    flat = grads.reshape(blocks * rows, columns)
    master, first, second, weights = step_call(
        dims, groups, stop, old_order, new_order, step, flat, master_old, moment_one_old, moment_two_old
    )
    return master[None], first[None], second[None], weights[None]


GROUPS = (((True, 4), (False, 4)), ((True, 5), (False, 5)))


def solution(mesh, dims=(4, 4, 2, 4, 18), groups=GROUPS, stop=0):
    return jax.shard_map(
        functools.partial(body, dims, groups, stop),
        mesh=mesh,
        in_specs=(
            P("shard", None, None),
            P("shard", None, None),
            P("shard", None, None),
            P("rep", "shard", None, None, None),
            P(),
            P(),
            P(),
        ),
        out_specs=(
            P("rep", "shard", None, None),
            P("rep", "shard", None, None),
            P("rep", "shard", None, None),
            P("rep", None, None, None),
        ),
        check_vma=False,
    )
```

```python
import functools
from types import SimpleNamespace

import jax
import jax.numpy as jnp
import numpy as np
from jax import lax
from jax.experimental import pallas as pl
from jax.experimental.pallas import tpu as pltpu
from jax.sharding import PartitionSpec as P

MESH = pl.DeviceIdType.MESH
LANES = 128
MARKS = 97
F32 = jnp.float32
BF16 = jnp.bfloat16


def power(base, count):
    out = jnp.float32(1.0)
    for bit in range(11):
        factor = np.float32(float(base) ** (1 << bit))
        taken = lax.rem(lax.shift_right_logical(count, jnp.int32(bit)), jnp.int32(2)) == 1
        out = jnp.where(taken, out * factor, out)
    return jnp.where(count >= 2048, jnp.float32(0.0), out)


def kernel(
    dims, groups, stop,
    old_in, new_in, step_in, grads, master, first, second,
    gathered, pairs, new_out,
    old_ref, new_ref, step_ref,
    state, state_out, cand, turn, owned,
    sems, *buffers,
):
    nx, ny, nzh, nzl, tiles = dims
    nz, ns, nb = nzh * nzl, nzh * nx, ny // 2
    half = tiles * LANES

    rep, shard = lax.axis_index("rep"), lax.axis_index("shard")
    core = lax.rem(rep, 2)
    y = lax.rem(lax.div(rep, 2), ny)
    zl = lax.div(rep, 2 * ny)
    x, zh = lax.rem(shard, nx), lax.div(shard, nx)
    z = zh * nzl + zl

    def device(x=x, y=y, zh=zh, zl=zl, core=core):
        return ((zl * ny + y) * 2 + core, zh * nx + x)

    def on_x(to):
        return device(x=to)

    def on_y(to):
        return device(y=to)

    def ahead(value, by, size):
        return lax.rem(value + by, size)

    used = []
    ends = []

    def mark():
        used.append(1)
        return sems.at[len(used) - 1]

    def take(ref, sem):
        pltpu.make_async_copy(ref, ref, sem).wait()

    def remote(src, dst, to, send, recv, when=None):
        copy = pltpu.make_async_remote_copy(
            src_ref=src, dst_ref=dst, send_sem=send, recv_sem=recv, device_id=to, device_id_type=MESH
        )
        if when is None:
            copy.start()
        else:
            pl.when(when)(copy.start)

    def local(src, dst, sem):
        copy = pltpu.make_async_copy(src, dst, sem)
        copy.start()
        return copy

    def sends(ref, when=None):
        sem = mark()
        ends.append((ref, sem, when))
        return sem

    def finish():
        for ref, sem, when in ends:
            if when is None:
                take(ref, sem)
            else:
                pl.when(when)(functools.partial(take, ref, sem))

    far = lambda n: sorted(range(1, n), key=lambda d: -min(d, n - d))
    mine = pl.multiple_of(core * half, LANES)
    theirs = pl.multiple_of((1 - core) * half, LANES)
    sibling = device(core=1 - core)

    teams, column, k = [], 0, 0
    for chunks in groups:
        g = SimpleNamespace(at=column, parts=[], tiles=sum(n for _, n in chunks))
        inner = 0
        for along_x, count_tiles in chunks:
            p = SimpleNamespace(along_x=along_x, at=column + inner, inner=inner, size=count_tiles * LANES)
            p.own, p.sib, p.chip, p.send, p.relay, p.recv1, p.part, p.recv2 = buffers[k:k + 8]
            k += 8
            p.n1, p.n2, p.me1, p.me2 = (nx, ny, x, y) if along_x else (ny, nx, y, x)
            p.to1, p.to2 = (on_x, on_y) if along_x else (on_y, on_x)
            inner += count_tiles * LANES
            g.parts.append(p)
        g.sum, g.recv3, g.result, g.result_z, g.short, g.short_z, g.wide, g.pair = buffers[k:k + 8]
        k += 8
        g.size = inner
        g.width = g.result.shape[2]
        g.fold = g.short.shape[1]
        g.starts = [(q * g.tiles // nzl) * LANES for q in range(nzl + 1)]
        column += inner
        teams.append(g)

    def piece(g, q):
        return pl.multiple_of(lax.div(q * g.tiles, nzl) * LANES, LANES)

    small = [local(src, dst, mark()) for src, dst in ((old_in, old_ref), (new_in, new_ref), (step_in, step_ref))]
    for g in teams:
        for p in g.parts:
            p.load = local(grads.at[:, pl.ds(mine + p.at, p.size)], p.own, mark())
    state_mark, column = mark(), 0
    for g in teams:
        g.state_at = column
        for a, ref in enumerate((master, first, second)):
            spot = pl.ds(mine + g.at + piece(g, zl), g.width)
            local(ref.at[:, :, spot], state.at[a, :, :, pl.ds(column, g.width)], state_mark)
        column += g.width

    partners = [sibling]
    partners += [device(x=ahead(x, d, nx)) for d in range(1, nx)]
    for d in range(1, ny):
        partners += [device(y=ahead(y, d, ny)), device(y=ahead(y, d, ny), core=1 - core)]
    for d in range(1, nz):
        other = ahead(z, d, nz)
        partners.append(device(zh=lax.div(other, nzl), zl=lax.rem(other, nzl)))
    for e in range(1, nzh):
        partners += [device(x=ahead(x, d, nx), zh=ahead(zh, e, nzh)) for d in range(1, nx)]
    barrier = pltpu.get_barrier_semaphore()
    for partner in partners:
        pl.semaphore_signal(barrier, inc=1, device_id=partner, device_id_type=MESH)
    pl.semaphore_wait(barrier, len(partners))

    swap_send = sends(grads.at[:, pl.ds(0, half)])

    def swap(g):
        for p in g.parts:
            p.swap = mark()
            remote(grads.at[:, pl.ds(theirs + p.at, p.size)], p.sib, sibling, swap_send, p.swap)


    holds = y < 3
    kind = jnp.where(holds, y, 2)
    moved = state_out.at[pl.ds(1, ns - 1)]
    move_send, move_recv = sends(moved, holds), mark()
    turn_marks = [mark() for _ in range(3)]
    turn_send = mark()
    turn_recv = sems.at[kind + (len(used) - 4)]
    ends.append((turn.at[pl.ds(0, ny - 1)], turn_send, holds))

    def state_first():
        take(state, state_mark)
        for e in range(nzh - 1, -1, -1):
            for d in far(nx) + [0]:
                to_x, to_zh = ahead(x, d, nx), ahead(zh, e, nzh)
                to_slot = (to_zh * nx + to_x) * ny
                pick = jnp.int32(0)
                for j in range(1, ny):
                    block = old_ref[shard * ny + j]
                    for q in range(ny):
                        pick = jnp.where(new_ref[to_slot + q] == block, jnp.int32(j), pick)
                slot = e * nx + d
                target = state_out if slot else cand
                target[slot] = state[kind, pick]
                if slot:
                    to = device(x=to_x, zh=to_zh)
                    remote(state_out.at[slot], cand.at[slot], to, move_send, move_recv, holds)

    def state_second():
        picks = []
        for q in range(ny):
            wanted = new_ref[shard * ny + q]
            pick = jnp.int32(0)
            for e in range(nzh):
                for d in range(nx):
                    if e or d:
                        from_x, from_zh = ahead(x, nx - d, nx), ahead(zh, nzh - e, nzh)
                        for j in range(ny):
                            match = old_ref[(from_zh * nx + from_x) * ny + j] == wanted
                            pick = jnp.where(match, jnp.int32(e * nx + d), pick)
            picks.append(pick)
        pl.when(holds)(functools.partial(take, moved, move_recv))
        for q in range(ny):
            turn[q] = cand[picks[q]]
            away = jnp.logical_and(holds, y != q)
            remote(turn.at[q], owned.at[kind], device(y=q), turn_send, turn_recv, away)

        @pl.when(holds)
        def _():
            owned[kind] = turn[y]

    def state_done():
        for a in range(3):
            pl.when(y != a)(functools.partial(take, owned.at[a], turn_marks[a]))

    def chip_sum(p):
        p.load.wait()
        take(p.sib, p.swap)

        def add(i, carry):
            rows = pl.ds(pl.multiple_of(i * 16, 16), 16)
            both = p.own[rows, :].astype(F32) + p.sib[rows, :].astype(F32)
            p.chip[2 * i] = both[:8]
            p.chip[2 * i + 1] = both[8:]
            return carry

        lax.fori_loop(0, ns * ny // 2, add, 0, unroll=8)

    def order(p, lead):
        for inner in range(p.n2):
            for e in range(nzh):
                to_x, to_y = (lead, inner) if p.along_x else (inner, lead)
                p.send[lead, inner, e] = p.chip[new_ref[(e * nx + to_x) * ny + to_y]]

    def first_step(p):
        chip_sum(p)
        n, me, h = p.n1, p.me1, p.n2 // 2
        low, high = pl.ds(0, h), pl.ds(h, h)
        up, down = ahead(me, 1, n), ahead(me, n - 1, n)
        if n == 2:
            order(p, up)
            p.got = mark()
            remote(p.send.at[up], p.recv1.at[0], p.to1(up), sends(p.send.at[0]), p.got)
            order(p, me)
            return
        to_up, to_down = p.to1(up), p.to1(down)
        across = ahead(me, 2, n)
        order(p, across)
        p.relays, p.got, p.out = [mark(), mark()], mark(), sends(p.send.at[pl.ds(0, 3)])
        out, got = p.out, p.got
        remote(p.send.at[across, low], p.relay.at[0], to_up, out, p.relays[0])
        remote(p.send.at[across, high], p.relay.at[1], to_down, out, p.relays[1])
        order(p, up)
        remote(p.send.at[up, high], p.recv1.at[0, high], to_up, out, got)
        order(p, down)
        remote(p.send.at[down, low], p.recv1.at[1, low], to_down, out, got)
        order(p, me)

    def second_step(p):
        n, me, h = p.n1, p.me1, p.n2 // 2
        if n == 2:
            return
        low, high = pl.ds(0, h), pl.ds(h, h)
        up, down = ahead(me, 1, n), ahead(me, n - 1, n)
        to_up, to_down = p.to1(up), p.to1(down)
        take(p.relay.at[0], p.relays[0])
        p.send[up, low] = p.send[up, low] + p.relay[0]
        remote(p.send.at[up, low], p.recv1.at[0, low], to_up, p.out, p.got)
        take(p.relay.at[1], p.relays[1])
        p.send[down, high] = p.send[down, high] + p.relay[1]
        remote(p.send.at[down, high], p.recv1.at[1, high], to_down, p.out, p.got)

    def third_step(p):
        take(p.recv1, p.got)
        p.second, out = mark(), sends(p.recv2)
        for d in far(p.n2) + [0]:
            to = ahead(p.me2, d, p.n2)
            for e in range(nzh):
                total = p.send[p.me1, to, e]
                for q in range(min(p.n1 - 1, 2)):
                    total = total + p.recv1[q, to, e]
                p.part[to, e] = total
            if d:
                remote(p.part.at[to], p.recv2.at[d - 1], p.to2(to), out, p.second)

    def sum_z(g):
        for p in g.parts:
            take(p.recv2, p.second)
            for e in range(nzh):
                total = p.part[p.me2, e]
                for q in range(p.n2 - 1):
                    total = total + p.recv2[q, e]
                g.sum[e, :, p.inner:p.inner + p.size] = total
        g.third, out = mark(), sends(g.recv3)
        for d in far(nz):
            other = ahead(z, d, nz)
            to_zh, to_zl = lax.div(other, nzl), lax.rem(other, nzl)
            src = g.sum.at[to_zh, :, pl.ds(piece(g, to_zl), g.width)]
            remote(src, g.recv3.at[d - 1], device(zh=to_zh, zl=to_zl), out, g.third)

    def update(g, fix_one, fix_two):
        take(g.recv3, g.third)
        grad = g.sum[zh, :, pl.ds(piece(g, zl), g.width)]
        for q in range(nz - 1):
            grad = grad + g.recv3[q]
        spot = slice(g.state_at, g.state_at + g.width)
        weight = owned[0, :, spot]
        moment_one = 0.9 * owned[1, :, spot] + 0.1 * grad
        moment_two = 0.95 * owned[2, :, spot] + 0.05 * grad * grad
        direction = moment_one / fix_one / (jnp.sqrt(moment_two / fix_two) + 1e-08)
        updated = weight - 0.1 * (direction + 0.1 * weight)
        fold, short, short_z = g.fold, g.short, g.short_z
        rest = updated[:, fold:]
        if rest.shape[1] < fold:
            rest = jnp.concatenate([rest, jnp.zeros((8, fold - rest.shape[1]), F32)], axis=1)
        short[...] = jnp.concatenate([updated[:, :fold], rest], axis=0).astype(BF16)
        g.over_z, out = mark(), sends(short_z.at[pl.ds(0, nz - 1)])
        for d in far(nz):
            other = ahead(z, d, nz)
            to = device(zh=lax.div(other, nzl), zl=lax.rem(other, nzl))
            remote(short, short_z.at[z], to, out, g.over_z)
        short_z[z] = short[...]
        for a, value in enumerate((updated, moment_one, moment_two)):
            g.result[a] = value
            g.result_z[zl, a] = value

    every = pl.ds(0, ny)
    up, down = ahead(x, 1, nx), ahead(x, nx - 1, nx)

    def extent(g, of, rows):
        return gathered.at[of, rows, :, pl.ds(0, g.size)]

    def block_place(g, of_x, of_y):
        return gathered.at[of_x, of_y, :, pl.ds(mine + g.at, g.size)]

    def weights_y(g):
        take(g.short_z.at[pl.ds(0, nz - 1)], g.over_z)
        starts, fold = g.starts, g.fold
        for q in range(nzl):
            span = starts[q + 1] - starts[q]
            for low, high, top in ((0, min(span, fold), 0), (fold, span, 8)):
                if high > low:
                    rows = [g.short_z[e * nzl + q, :, :high - low].astype(F32)[top:top + 8] for e in range(nzh)]
                    g.wide[:, starts[q] + low:starts[q] + high] = jnp.concatenate(rows, axis=0).astype(BF16)
        place = block_place(g, x, y)
        g.over_y, out = mark(), sends(extent(g, 0, pl.ds(0, ny - 1)))
        g.out = sends(extent(g, pl.ds(0, 3), every))
        g.come, g.near, g.far = [mark() for _ in range(4)], mark(), mark()
        for d in far(ny):
            remote(g.wide, place, device(y=ahead(y, d, ny)), out, g.over_y)
        remote(g.wide, place, device(x=up), g.out, g.come[0])
        remote(g.wide, place, device(x=down), g.out, g.near)
        g.kept = local(g.wide, place, mark())

    def masters_z(g):
        g.over_zl = [mark() for _ in range(nzl)]
        landed = sems.at[len(used) - nzl + zl]
        if nzl > 1:
            out = sends(g.result_z.at[pl.ds(0, nzl - 1)])
        for d in far(nzl):
            remote(g.result, g.result_z.at[zl], device(zl=ahead(zl, d, nzl)), out, landed)

    member, row = lax.div(y, nb), lax.rem(y, nb)

    def hand_out(g, q, src, when):
        at, wide = g.starts[q], g.starts[q + 1] - g.starts[q]
        src = src.at[:, :, pl.ds(0, wide)]
        place = pairs.at[:, row, :, pl.ds(mine + g.at + at, wide)]
        for d in far(ny):
            remote(src, place, device(y=ahead(y, d, ny), core=member), g.pair_out, g.landed, when)
        remote(src, place, sibling, g.pair_give, g.landed, jnp.logical_and(when, member != core))
        within = pltpu.make_async_copy(src, place, g.landed)
        pl.when(jnp.logical_and(when, member == core))(within.start)

    def pairs_own(g):
        g.pair_marks = [mark() for _ in range(2 * nb)]
        g.landed = sems.at[len(used) - 2 * nb + row * 2 + core]
        g.pair_out = sends(pairs.at[:, 0, :, pl.ds(0, (ny - 1) * g.size)])
        g.pair_give = sends(g.pair, member != core)
        for q in range(nzl):
            hand_out(g, q, g.result, zl == q)

    def pairs_y(g):
        for q in range(nzl):
            pl.when(zl != q)(functools.partial(take, g.result_z.at[q], g.over_zl[q]))
            hand_out(g, q, g.result_z.at[q], zl != q)

    def pairs_done(g):
        for k in range(2 * nb):
            take(g.pair, g.pair_marks[k])

    def pass_on(g, of, rows, to, send, recv):
        place = gathered.at[of, rows, :, pl.ds(mine + g.at, g.size)]
        remote(place, place, to, send, recv)

    def weights_x(g):
        to_up, to_down = device(x=up), device(x=down)
        block = extent(g, 0, 0)
        rows = [ahead(y, j, ny) for j in range(ny)]
        take(extent(g, 0, pl.ds(0, ny - 1)), g.over_y)
        g.kept.wait()
        pass_on(g, x, rows[1], to_up, g.out, g.come[1])
        pass_on(g, x, rows[2], to_down, g.out, g.come[2])
        pass_on(g, x, rows[3], to_down, g.out, g.come[3])
        pass_on(g, x, rows[2], to_up, g.out, g.near)
        pass_on(g, x, rows[3], to_up, g.out, g.near)
        pass_on(g, x, rows[1], to_down, g.out, g.near)
        g.given, g.give = mark(), sends(extent(g, pl.ds(0, nx), every))
        pass_on(g, x, every, sibling, g.give, g.given)

    def weights_on(g):
        block = extent(g, 0, 0)
        rows = [ahead(y, j, ny) for j in range(ny)]
        take(block, g.come[0])
        pass_on(g, down, rows[0], device(x=up), g.out, g.far)
        take(block, g.come[1])
        pass_on(g, down, rows[1], device(x=up), g.out, g.far)
        take(block, g.come[2])
        pass_on(g, up, rows[2], device(x=down), g.out, g.far)
        take(block, g.come[3])
        pass_on(g, up, rows[3], device(x=down), g.out, g.far)

    def weights_last(g):
        take(extent(g, 0, every), g.near)
        pass_on(g, down, every, sibling, g.give, g.given)
        pass_on(g, up, every, sibling, g.give, g.given)
        take(extent(g, 0, every), g.far)
        pass_on(g, ahead(x, 2, nx), every, sibling, g.give, g.given)

    for copy in small:
        copy.wait()
    for k in range(ns * ny):
        new_out[k] = new_ref[k]
    one, two = teams
    (a0, b0), (a1, b1) = one.parts, two.parts
    swap(one)
    swap(two)
    state_first()
    first_step(a0)
    first_step(b0)
    first_step(a1)
    first_step(b1)
    second_step(a0)
    second_step(b0)
    t = step_ref[0]
    fix_one = 1.0 - power(0.9, t)
    fix_two = 1.0 - power(0.95, t)
    second_step(a1)
    second_step(b1)
    state_second()
    third_step(a0)
    third_step(b0)
    third_step(a1)
    third_step(b1)
    sum_z(one)
    sum_z(two)
    state_done()
    update(one, fix_one, fix_two)
    update(two, fix_one, fix_two)
    weights_y(one)
    pairs_own(one)
    masters_z(one)
    weights_y(two)
    pairs_own(two)
    masters_z(two)
    weights_x(one)
    weights_x(two)
    pairs_y(one)
    weights_on(one)
    pairs_y(two)
    weights_on(two)
    weights_last(one)
    weights_last(two)
    for g in teams:
        pairs_done(g)
        take(extent(g, pl.ds(0, nx), every), g.given)
    finish()


def spread_kernel(dims, new_ref, gathered, pairs, master_out, first_out, second_out, weights_out, sem):
    nx, ny, nzh, _, _ = dims
    copies = []
    for a, ref in enumerate((master_out, first_out, second_out)):
        copies.append(pltpu.make_async_copy(pairs.at[a], ref, sem.at[1 + a]))
        copies[-1].start()
    for k in range(nzh * nx * ny):
        e, at_x, at_y = k // (nx * ny), k // ny % nx, k % ny
        copy = (
            pltpu.make_async_copy(gathered.at[(at_x * ny + at_y) * nzh + e], weights_out.at[new_ref[k]], sem.at[4])
        )
        copy.start()
    for copy in copies:
        copy.wait()
    pltpu.make_async_copy(gathered, gathered, sem.at[4]).wait()


def step_call(dims, groups, stop, old_order, new_order, step, grads, master, first, second):
    nx, ny, nzh, nzl, tiles = dims
    nz, ns, nb = nzh * nzl, nzh * nx, ny // 2
    half = tiles * LANES
    blocks = ns * ny
    vmem = pltpu.VMEM
    anywhere = pl.BlockSpec(memory_space=pl.ANY)
    scalars = pl.BlockSpec(memory_space=pltpu.SMEM)
    outside = pl.BlockSpec(memory_space=pltpu.HBM)
    inside = pl.BlockSpec(memory_space=pltpu.VMEM)
    buffers, state_width = [], 0
    for chunks in groups:
        for along_x, count_tiles in chunks:
            n1, n2 = (nx, ny) if along_x else (ny, nx)
            size = count_tiles * LANES
            buffers += [
                vmem((8 * blocks, size), BF16),
                vmem((8 * blocks, size), BF16),
                vmem((blocks, 8, size), F32),
                vmem((n1, n2, nzh, 8, size), F32),
                vmem((2, n2 // 2, nzh, 8, size), F32),
                vmem((min(n1 - 1, 2), n2, nzh, 8, size), F32),
                vmem((n2, nzh, 8, size), F32),
                vmem((n2 - 1, nzh, 8, size), F32),
            ]
        group_tiles = sum(n for _, n in chunks)
        size = group_tiles * LANES
        width = -(-group_tiles // nzl) * LANES
        fold = -(-width // (2 * LANES)) * LANES
        state_width += width
        buffers += [
            vmem((nzh, 8, size), F32),
            vmem((nz - 1, 8, width), F32),
            vmem((3, 8, width), F32),
            vmem((nzl, 3, 8, width), F32),
            vmem((16, fold), BF16),
            vmem((nz, 16, fold), BF16),
            vmem((8 * nzh, size), BF16),
            vmem((3, 8, size), F32),
        ]
    gathered, pairs, kept = pl.pallas_call(
        functools.partial(kernel, dims, groups, stop),
        out_shape=(pltpu.VMEM((nx, ny, 8 * nzh, 2 * half), BF16), pltpu.VMEM((3, nb, 8, 2 * half), F32), pltpu.SMEM((blocks,), jnp.int32)),
        in_specs=[anywhere] * 3 + [outside] * 4,
        out_specs=[inside] * 2 + [scalars],
        scratch_shapes=[
            pltpu.SMEM((blocks,), jnp.int32),
            pltpu.SMEM((blocks,), jnp.int32),
            pltpu.SMEM((1,), jnp.int32),
            vmem((3, ny, 8, state_width), F32),
            vmem((ns, 8, state_width), F32),
            vmem((ns, 8, state_width), F32),
            vmem((ny, 8, state_width), F32),
            vmem((3, 8, state_width), F32),
            pltpu.SemaphoreType.DMA((MARKS,)),
        ] + buffers,
        compiler_params=pltpu.CompilerParams(
            collective_id=0, has_side_effects=True, vmem_limit_bytes=60 * 1024 * 1024
        ),
        cost_estimate=pl.CostEstimate(flops=4_000_000, bytes_accessed=8_000_000, transcendentals=0),
    )(old_order, new_order, step, grads, master, first, second)
    f32_out = jax.ShapeDtypeStruct((nb, 8, 2 * half), F32)
    return pl.pallas_call(
        functools.partial(spread_kernel, dims),
        out_shape=(f32_out, f32_out, f32_out, jax.ShapeDtypeStruct((blocks, 8, 2 * half), BF16)),
        in_specs=[scalars, inside, inside],
        out_specs=[anywhere] * 4,
        scratch_shapes=[pltpu.SemaphoreType.DMA((5,))],
        compiler_params=pltpu.CompilerParams(vmem_limit_bytes=8 * 1024 * 1024),
    )(kept, gathered.reshape(blocks, 8, 2 * half), pairs)


def body(dims, groups, stop, master_old, moment_one_old, moment_two_old, grads, old_order, new_order, step):
    blocks, rows, columns = grads.shape[2:]
    flat = grads.reshape(blocks * rows, columns)
    master, first, second, weights = step_call(
        dims, groups, stop, old_order, new_order, step, flat, master_old, moment_one_old, moment_two_old
    )
    return master[None], first[None], second[None], weights[None]


GROUPS = (((True, 4), (False, 4)), ((True, 5), (False, 5)))


def solution(mesh, dims=(4, 4, 2, 4, 18), groups=GROUPS, stop=0):
    return jax.shard_map(
        functools.partial(body, dims, groups, stop),
        mesh=mesh,
        in_specs=(
            P("shard", None, None),
            P("shard", None, None),
            P("shard", None, None),
            P("rep", "shard", None, None, None),
            P(),
            P(),
            P(),
        ),
        out_specs=(
            P("rep", "shard", None, None),
            P("rep", "shard", None, None),
            P("rep", "shard", None, None),
            P("rep", None, None, None),
        ),
        check_vma=False,
    )
```
